128 devices in a mesh: dp: 32 (over y, x, core), pipe: 4 (over z).
Axes of the slice: x: 4, y: 4, z: 4, core: 2. Of those that a mesh axis runs over, the one named last changes fastest.
Arguments:
- latents: bfloat16 [96, 192, 320], P('dp'), may hold values from -6 to 6
- cotangent: bfloat16 [96, 192, 320], P('dp'), may hold values from -0.109375 to 0.109375
- timesteps: int32 [96], P('dp'), may hold values from 0 to 999
- layer_count: int32 [4], P('pipe'), may hold values from 1 to 3, as said below
- up_weight: bfloat16 [4, 3, 320, 1280], P('pipe'), may hold values from -0.3125 to 0.3125
- down_weight: bfloat16 [4, 3, 1280, 320], P('pipe'), may hold values from -0.15625 to 0.15625
- time_weight: bfloat16 [4, 3, 320, 640], P('pipe'), may hold values from -0.3125 to 0.3125
- skip_weight: bfloat16 [4, 320, 320], P('pipe'), may hold values from -0.3125 to 0.3125
Outputs:
- grad_up: float32 [4, 3, 320, 1280], P('pipe', None, 'dp')
- grad_down: float32 [4, 3, 1280, 320], P('pipe', None, 'dp')
- grad_time: float32 [4, 3, 320, 640], P('pipe', None, 'dp')
- grad_skip: float32 [4, 320, 320], P('pipe', 'dp')
The draws below stay inside these ranges and needn't reach their ends.
Inputs may be any that keep to these rules, and one draw needn't show every extreme that they name: `layer_count`: some section runs all 3 layer slots and some section runs only one.
All inputs are finite; a program needn't handle non-finite values.
Results may differ from the reference program's by a relative error of at most 0.033.
Values may be sent and summed in bfloat16 or wider, within the bound.
No kernel may reach another device: no remote copies, remote signals or barrier semaphores. Data moves between devices by JAX's collectives and lax.ppermute only.
A program may use at most 192 MiB of HBM per device.

```python
import math
import jax
import jax.numpy as jnp
from jax import lax

D = 320
FF = 1280
TEMB = 320
ROWS = 192
SLOTS = 3
SECTIONS = 4
SAMPLES = 96


def draw_layer_count(key, part):
    first_key, second_key = jax.random.split(key, 2)
    counts = jax.random.randint(first_key, (SECTIONS,), 1, SLOTS + 1)
    order = jax.random.permutation(second_key, SECTIONS)
    positions = jnp.arange(SECTIONS)
    counts = jnp.where(positions == order[0], SLOTS, counts)
    counts = jnp.where(positions == order[1], 1, counts)
    return counts.astype(jnp.int32)


def place_ends(values, key, smallest, top_value):
    shape = values.shape
    place = [jax.random.randint(jax.random.fold_in(key, axis), (), 0, shape[axis]) for axis in range(len(shape))]
    values = values.at[tuple(place)].set(smallest)
    longest = shape.index(max(shape))
    place[longest] = (place[longest] + 1) % shape[longest]
    return values.at[tuple(place)].set(top_value)


def levels(key, shape, cuts, least, largest):
    level, own = 1.0, jax.random.fold_in(key, 6)
    for dim, blocks in cuts:
        draws = jnp.exp(jax.random.uniform(jax.random.fold_in(own, dim), (blocks,), jnp.float32, least / len(cuts), largest / len(cuts)))
        level = level * jnp.repeat(draws, shape[dim] // blocks).reshape([-1 if axis == dim else 1 for axis in range(len(shape))])
    return level


def centred(own_key, shape, deviation, limit, shards=(), kind=jnp.bfloat16):
    array = deviation * jax.random.normal(own_key, shape, jnp.float32)
    if shards:
        array = array * levels(own_key, shape, shards, -0.22, 0.18)
    return jnp.clip(array, -limit, limit).astype(kind)


def setup_inputs(seed: int = 0) -> dict:
    splits = jax.random.split(jax.random.key(seed), 9)
    latents = centred(splits[0], (SAMPLES, ROWS, D), 1.0, 6.0, ((0, 32),))
    cotangent = centred(splits[1], (SAMPLES, ROWS, D), ((SAMPLES * ROWS) ** -0.5), 0.109375, ((0, 32),))
    timesteps = place_ends(jax.random.randint(splits[2], (SAMPLES,), 0, 1000), jax.random.fold_in(splits[2], 1), 0, 999).astype(jnp.int32)
    layer_count = draw_layer_count(jax.random.fold_in(splits[8], 71), 0)
    up_weight = centred(splits[4], (SECTIONS, SLOTS, D, FF), D ** -0.5, 0.3125, ((0, 4),))
    down_weight = centred(splits[5], (SECTIONS, SLOTS, FF, D), FF ** -0.5, 0.15625, ((0, 4),))
    time_weight = centred(splits[6], (SECTIONS, SLOTS, TEMB, 2 * D), TEMB ** -0.5, 0.3125, ((0, 4),))
    skip_weight = centred(splits[7], (SECTIONS, D, D), D ** -0.5, 0.3125, ((0, 4),))
    return {"latents": latents, "cotangent": cotangent, "timesteps": timesteps, "layer_count": layer_count, "up_weight": up_weight, "down_weight": down_weight, "time_weight": time_weight, "skip_weight": skip_weight}


EPSILON = 1e-06

def embedding(timesteps):
    halfway = TEMB // 2
    frequency = jnp.exp(-math.log(10000.0) * jnp.arange(halfway, dtype=jnp.float32) / halfway)
    angles = timesteps.astype(jnp.float32)[..., None] * frequency
    return jnp.concatenate([jnp.sin(angles), jnp.cos(angles)], axis=-1)

def apply_layer(state, modulation, up_matrix, down_matrix):
    channels = state.shape[-1]
    scaling = modulation[:channels]
    offset = modulation[channels:]
    inverse = lax.rsqrt(lax.optimization_barrier(jnp.mean(state * state, axis=-1, keepdims=True)) + EPSILON)
    normed = (state * inverse * (1.0 + scaling) + offset).astype(jnp.bfloat16)
    hidden = jax.nn.silu(jnp.dot(normed, up_matrix, preferred_element_type=jnp.float32)).astype(jnp.bfloat16)
    return state + jnp.dot(hidden, down_matrix, preferred_element_type=jnp.float32)

def network(inputs, modulation, up_weight, down_weight, skip_weight, layer_count):
    outputs = []
    carried = inputs
    for section_number in range(SECTIONS):
        state = carried.astype(jnp.float32)
        if section_number >= SECTIONS // 2:
            state = state + jnp.dot(outputs[SECTIONS - 1 - section_number], skip_weight[section_number], preferred_element_type=jnp.float32)
        for layer_slot in range(SLOTS):
            updated = apply_layer(state, modulation[section_number, layer_slot], up_weight[section_number, layer_slot], down_weight[section_number, layer_slot])
            state = jnp.where(layer_slot < layer_count[section_number], updated, state)
        carried = state.astype(jnp.bfloat16)
        outputs.append(carried)
    return carried

def reference(latents, cotangent, timesteps, layer_count, up_weight, down_weight, time_weight, skip_weight):
    conditioning = jax.nn.silu(embedding(timesteps)).astype(jnp.bfloat16)
    time_wide = time_weight.astype(jnp.float32)

    def one_sample(totals, sample):
        inputs, tangent, condition = sample
        condition_wide = condition.astype(jnp.float32)
        modulation = jnp.einsum('t,sjtc->sjc', condition_wide, time_wide)

        def forward(up_part, down_part, skip_part, mod_part):
            return network(inputs, mod_part, up_part, down_part, skip_part, layer_count)
        _, pullback = jax.vjp(forward, up_weight, down_weight, skip_weight, modulation)
        sample_up, sample_down, sample_skip, mod_grads = pullback(tangent)
        time_terms = (condition_wide[None, None, :, None] * mod_grads[:, :, None, :]).astype(jnp.bfloat16)
        time_terms = lax.optimization_barrier(time_terms).astype(jnp.float32)
        updated = (totals[0] + sample_up.astype(jnp.float32), totals[1] + sample_down.astype(jnp.float32), totals[2] + time_terms, totals[3] + sample_skip.astype(jnp.float32))
        return (updated, None)
    start = (jnp.zeros(up_weight.shape, jnp.float32), jnp.zeros(down_weight.shape, jnp.float32), jnp.zeros(time_weight.shape, jnp.float32), jnp.zeros(skip_weight.shape, jnp.float32))
    totals, _ = lax.scan(one_sample, start, (latents, cotangent, conditioning))
    return (totals[0], totals[1], totals[2], totals[3])
```

```python
import functools
import math

import jax
import jax.numpy as jnp
import ml_dtypes
import numpy as np
from jax import lax
from jax.experimental import pallas as pl
from jax.experimental.pallas import tpu as pltpu
from jax.sharding import Mesh
from jax.sharding import PartitionSpec as P

EPSILON = 1e-06
BF16 = jnp.bfloat16
F32 = jnp.float32
CHUNK = 256
VMEM_LIMIT = 40 * 1024 * 1024
ANY = pl.BlockSpec(memory_space=pl.ANY)
SMEM = pl.BlockSpec(memory_space=pltpu.SMEM)
NT = (((1,), (1,)), ((), ()))
TN = (((0,), (0,)), ((), ()))


def embedding(timesteps, halfway):
    frequency = jnp.exp(-math.log(10000.0) * jnp.arange(halfway, dtype=F32) / halfway)
    angles = timesteps.astype(F32)[..., None] * frequency
    return jnp.concatenate([jnp.sin(angles), jnp.cos(angles)], axis=-1)


def nt_dot(left, right):
    return lax.dot_general(left, right, NT, preferred_element_type=F32)


def sigmoid(value):
    return 0.5 * jnp.tanh(0.5 * value) + 0.5


def copies_in(pairs, sems):
    return [pltpu.make_async_copy(src, dst, sems.at[i]) for i, (src, dst) in enumerate(pairs)]


def forward_kernel(tick, has_saved, has_skip, samples, slots, sections, width, *refs):
    refs = list(refs)
    scal, mod, latents, incoming, up, down, skip_weight = refs[:7]
    del refs[:7]
    skip_in = refs.pop(0) if has_skip else None
    if has_saved:
        del refs[:3]
    out, states, pres, skips = refs[:4]
    xv, sv, modv, upv, downv, skwv, statev, prev, acc, sems = refs[4:]
    stage, count = scal[0], scal[1]
    sample = tick - 2 * stage
    hidden_width = upv.shape[2]
    half = sections // 2

    @pl.when((sample >= 0) & (sample < samples))
    def _():
        copy_latents = pltpu.make_async_copy(latents.at[sample], xv, sems.at[0])
        copy_incoming = pltpu.make_async_copy(incoming, xv, sems.at[0])
        copy_mod = pltpu.make_async_copy(mod.at[sample], modv, sems.at[1])
        copy_skw = pltpu.make_async_copy(skip_weight, skwv, sems.at[2])
        copy_up = copies_in([(up.at[j], upv.at[j]) for j in range(slots)], sems.at[pl.ds(4, slots)])
        copy_down = copies_in(
            [(down.at[j], downv.at[j]) for j in range(slots)], sems.at[pl.ds(4 + slots, slots)]
        )
        save_state = copies_in(
            [(statev.at[j], states.at[sample, j]) for j in range(slots)],
            sems.at[pl.ds(4 + 2 * slots, slots)],
        )
        save_pre = copies_in(
            [(prev.at[j], pres.at[sample, j]) for j in range(slots)],
            sems.at[pl.ds(4 + 3 * slots, slots)],
        )
        save_skip = pltpu.make_async_copy(sv, skips.at[sample], sems.at[3])

        @pl.when(stage == 0)
        def _():
            copy_latents.start()

        @pl.when(stage != 0)
        def _():
            copy_incoming.start()

        copy_mod.start()
        decoder = stage >= half

        @pl.when(decoder)
        def _():
            copy_skw.start()

        for j in range(slots):

            @pl.when(j < count)
            def _():
                copy_up[j].start()
                copy_down[j].start()

        copy_incoming.wait()
        acc[...] = xv[...].astype(F32)

        @pl.when(decoder)
        def _():
            if has_skip:
                copy_skip = pltpu.make_async_copy(skip_in, sv, sems.at[3])

                @pl.when(stage == sections - 1)
                def _():
                    copy_skip.start()
                    copy_skip.wait()

                @pl.when(stage != sections - 1)
                def _():
                    sv[...] = xv[...]

            else:
                sv[...] = xv[...]
            save_skip.start()
            copy_skw.wait()
            acc[...] += jnp.dot(sv[...], skwv[...], preferred_element_type=F32)

        copy_mod.wait()
        for j in range(slots):

            @pl.when(j < count)
            def _():
                state = acc[...]
                statev[j] = state
                save_state[j].start()
                scaling = modv[j : j + 1, :width]
                offset = modv[j : j + 1, width:]
                inverse = lax.rsqrt(jnp.mean(state * state, axis=-1, keepdims=True) + EPSILON)
                normed = (state * inverse * (1.0 + scaling) + offset).astype(BF16)
                copy_up[j].wait()
                copy_down[j].wait()
                total = state
                for start in range(0, hidden_width, CHUNK):
                    cols = slice(start, start + CHUNK)
                    pre = jnp.dot(normed, upv[j, :, cols], preferred_element_type=F32)
                    prev[j, :, cols] = pre.astype(BF16)
                    hidden = (pre * sigmoid(pre)).astype(BF16)
                    total = total + jnp.dot(hidden, downv[j, cols, :], preferred_element_type=F32)
                acc[...] = total
                save_pre[j].start()

        xv[...] = acc[...].astype(BF16)
        save_out = pltpu.make_async_copy(xv, out, sems.at[0])
        save_out.start()
        for j in range(slots):

            @pl.when(j < count)
            def _():
                save_state[j].wait()
                save_pre[j].wait()

        @pl.when(decoder)
        def _():
            save_skip.wait()

        save_out.wait()


def forward_call(tick, scal, mod, latents, incoming, up, down, skip_weight, skip_in, saved):
    samples, rows, width = latents.shape
    slots, _, hidden_width = up.shape
    shapes = (
        jax.ShapeDtypeStruct((rows, width), BF16),
        jax.ShapeDtypeStruct((samples, slots, rows, width), F32),
        jax.ShapeDtypeStruct((samples, slots, rows, hidden_width), BF16),
        jax.ShapeDtypeStruct((samples, rows, width), BF16),
    )
    operands = [scal, mod, latents, incoming, up, down, skip_weight]
    if skip_in is not None:
        operands.append(skip_in)
    aliases = {}
    if saved is not None:
        aliases = {len(operands) + i: 1 + i for i in range(3)}
        operands += list(saved)
    out = pl.pallas_call(
        functools.partial(
            forward_kernel,
            tick,
            saved is not None,
            skip_in is not None,
            samples,
            slots,
            4,
            width,
        ),
        out_shape=shapes,
        in_specs=[SMEM] + [ANY] * (len(operands) - 1),
        out_specs=(ANY,) * 4,
        input_output_aliases=aliases,
        scratch_shapes=[
            pltpu.VMEM((rows, width), BF16),
            pltpu.VMEM((rows, width), BF16),
            pltpu.VMEM((slots, 2 * width), F32),
            pltpu.VMEM((slots, width, hidden_width), BF16),
            pltpu.VMEM((slots, hidden_width, width), BF16),
            pltpu.VMEM((width, width), BF16),
            pltpu.VMEM((slots, rows, width), F32),
            pltpu.VMEM((slots, rows, hidden_width), BF16),
            pltpu.VMEM((rows, width), F32),
            pltpu.SemaphoreType.DMA((4 + 4 * slots,)),
        ],
        compiler_params=pltpu.CompilerParams(vmem_limit_bytes=VMEM_LIMIT),
        cost_estimate=pl.CostEstimate(
            flops=slots * rows * width * hidden_width * 4,
            bytes_accessed=8_000_000,
            transcendentals=0,
        ),
        name=f"section_forward_{tick}",
    )(*operands)
    return out[0], out[1:]


def backward_kernel(tick, has_saved, has_skip, samples, slots, sections, width, *refs):
    refs = list(refs)
    scal, mod, cotangent, incoming, up, down, skip_weight, states, pres = refs[:9]
    del refs[:9]
    skip_grad = refs.pop(0) if has_skip else None
    if has_saved:
        del refs[:6]
    out, out_skip, norms, outs, hiddens, dpres, mod_grads, firsts = refs[:8]
    gv, hv, modv, upv, downv, skwv, statev, prev, acc, nv, ov, hidv, dpv, mgv, fv, sems = refs[8:]
    stage, count = scal[0], scal[1]
    sample = tick - 2 * (sections - 1 - stage)
    hidden_width = upv.shape[2]
    half = sections // 2

    @pl.when((sample >= 0) & (sample < samples))
    def _():
        copy_cot = pltpu.make_async_copy(cotangent.at[sample], gv, sems.at[0])
        copy_incoming = pltpu.make_async_copy(incoming, gv, sems.at[0])
        copy_mod = pltpu.make_async_copy(mod.at[sample], modv, sems.at[1])
        copy_skw = pltpu.make_async_copy(skip_weight, skwv, sems.at[2])

        def group(index, pairs):
            return copies_in(pairs, sems.at[pl.ds(4 + index * slots, slots)])

        each = range(slots)
        copy_up = group(0, [(up.at[j], upv.at[j]) for j in each])
        copy_down = group(1, [(down.at[j], downv.at[j]) for j in each])
        copy_state = group(2, [(states.at[sample, j], statev.at[j]) for j in each])
        copy_pre = group(3, [(pres.at[sample, j], prev.at[j]) for j in each])
        save_norm = group(4, [(nv.at[j], norms.at[j, sample]) for j in each])
        save_out = group(5, [(ov.at[j], outs.at[j, sample]) for j in each])
        save_hid = group(6, [(hidv.at[j], hiddens.at[j, sample]) for j in each])
        save_dpre = group(7, [(dpv.at[j], dpres.at[j, sample]) for j in each])

        @pl.when(stage == sections - 1)
        def _():
            copy_cot.start()

        @pl.when(stage != sections - 1)
        def _():
            copy_incoming.start()

        if has_skip:
            copy_skip = pltpu.make_async_copy(skip_grad, hv, sems.at[3])

            @pl.when(stage == 0)
            def _():
                copy_skip.start()

        copy_mod.start()
        decoder = stage >= half
        for j in reversed(each):

            @pl.when(j < count)
            def _():
                copy_down[j].start()
                copy_pre[j].start()
                copy_up[j].start()
                copy_state[j].start()

        @pl.when(decoder)
        def _():
            copy_skw.start()

        copy_incoming.wait()
        if has_skip:

            @pl.when(stage == 0)
            def _():
                copy_skip.wait()
                acc[...] = (gv[...] + hv[...]).astype(F32)

            @pl.when(stage != 0)
            def _():
                acc[...] = gv[...].astype(F32)

        else:
            acc[...] = gv[...].astype(F32)
        copy_mod.wait()
        mgv[...] = jnp.zeros_like(mgv)
        for j in reversed(each):

            @pl.when(j < count)
            def _():
                grad = acc[...]
                grad_b = grad.astype(BF16)
                ov[j] = grad_b
                save_out[j].start()
                copy_down[j].wait()
                copy_pre[j].wait()
                copy_up[j].wait()
                total = jnp.zeros(grad.shape, F32)
                for start in range(0, hidden_width, CHUNK):
                    cols = slice(start, start + CHUNK)
                    grad_hidden = nt_dot(grad_b, downv[j, cols, :])
                    pre = prev[j, :, cols].astype(F32)
                    gate = sigmoid(pre)
                    hidden = pre * gate
                    hidv[j, :, cols] = hidden.astype(BF16)
                    grad_pre = (grad_hidden * (gate + hidden * (1.0 - gate))).astype(BF16)
                    dpv[j, :, cols] = grad_pre
                    total = total + nt_dot(grad_pre, upv[j, :, cols])
                save_hid[j].start()
                save_dpre[j].start()
                copy_state[j].wait()
                state = statev[j]
                scaling = 1.0 + modv[j : j + 1, :width]
                offset = modv[j : j + 1, width:]
                inverse = lax.rsqrt(jnp.mean(state * state, axis=-1, keepdims=True) + EPSILON)
                unit = state * inverse
                nv[j] = (unit * scaling + offset).astype(BF16)
                save_norm[j].start()
                grad_norm = total.astype(BF16).astype(F32)
                scaled = grad_norm * unit
                mgv[j : j + 1, :width] = jnp.sum(scaled, axis=0, keepdims=True)
                mgv[j : j + 1, width:] = jnp.sum(grad_norm, axis=0, keepdims=True)
                inner = jnp.mean(scaled * scaling, axis=-1, keepdims=True)
                acc[...] = grad + inverse * (grad_norm * scaling - unit * inner)

        save_mods = pltpu.make_async_copy(mgv, mod_grads.at[sample], sems.at[1])
        save_mods.start()
        first = acc[...].astype(BF16)
        fv[...] = first
        gv[...] = first
        save_first = pltpu.make_async_copy(fv, firsts.at[sample], sems.at[3])
        save_first.start()

        @pl.when(decoder)
        def _():
            copy_skw.wait()
            grad_skip = nt_dot(first, skwv[...]).astype(BF16)
            hv[...] = grad_skip

            @pl.when(stage == half)
            def _():
                gv[...] = first + grad_skip

        save_down = pltpu.make_async_copy(gv, out, sems.at[0])
        save_skip = pltpu.make_async_copy(hv, out_skip, sems.at[2])
        save_down.start()

        @pl.when(stage == sections - 1)
        def _():
            save_skip.start()
            save_skip.wait()

        for j in each:

            @pl.when(j < count)
            def _():
                save_norm[j].wait()
                save_out[j].wait()
                save_hid[j].wait()
                save_dpre[j].wait()

        save_first.wait()
        save_mods.wait()
        save_down.wait()


def backward_call(
    tick, scal, mod, cotangent, incoming, up, down, skip_weight, states, pres, skip_grad, saved
):
    samples, rows, width = cotangent.shape
    slots, _, hidden_width = up.shape
    narrow = (rows, width)
    wide = (rows, hidden_width)
    shapes = (
        jax.ShapeDtypeStruct(narrow, BF16),
        jax.ShapeDtypeStruct(narrow, BF16),
        jax.ShapeDtypeStruct((slots, samples, *narrow), BF16),
        jax.ShapeDtypeStruct((slots, samples, *narrow), BF16),
        jax.ShapeDtypeStruct((slots, samples, *wide), BF16),
        jax.ShapeDtypeStruct((slots, samples, *wide), BF16),
        jax.ShapeDtypeStruct((samples, slots, 2 * width), F32),
        jax.ShapeDtypeStruct((samples, *narrow), BF16),
    )
    operands = [scal, mod, cotangent, incoming, up, down, skip_weight, states, pres]
    if skip_grad is not None:
        operands.append(skip_grad)
    aliases = {}
    if saved is not None:
        aliases = {len(operands) + i: 2 + i for i in range(6)}
        operands += list(saved)
    out = pl.pallas_call(
        functools.partial(
            backward_kernel,
            tick,
            saved is not None,
            skip_grad is not None,
            samples,
            slots,
            4,
            width,
        ),
        out_shape=shapes,
        in_specs=[SMEM] + [ANY] * (len(operands) - 1),
        out_specs=(ANY,) * len(shapes),
        input_output_aliases=aliases,
        scratch_shapes=[
            pltpu.VMEM(narrow, BF16),
            pltpu.VMEM(narrow, BF16),
            pltpu.VMEM((slots, 2 * width), F32),
            pltpu.VMEM((slots, width, hidden_width), BF16),
            pltpu.VMEM((slots, hidden_width, width), BF16),
            pltpu.VMEM((width, width), BF16),
            pltpu.VMEM((slots, *narrow), F32),
            pltpu.VMEM((slots, *wide), BF16),
            pltpu.VMEM(narrow, F32),
            pltpu.VMEM((slots, *narrow), BF16),
            pltpu.VMEM((slots, *narrow), BF16),
            pltpu.VMEM((slots, *wide), BF16),
            pltpu.VMEM((slots, *wide), BF16),
            pltpu.VMEM((slots, 2 * width), F32),
            pltpu.VMEM(narrow, BF16),
            pltpu.SemaphoreType.DMA((4 + 8 * slots,)),
        ],
        compiler_params=pltpu.CompilerParams(vmem_limit_bytes=VMEM_LIMIT),
        cost_estimate=pl.CostEstimate(
            flops=slots * rows * width * hidden_width * 4,
            bytes_accessed=14_000_000,
            transcendentals=0,
        ),
        name=f"section_backward_{tick}",
    )(*operands)
    return out[0], out[1], out[2:]


def up_grad_kernel(scal, norm, dpre, order, mine, theirs, product):
    count, core = scal[1], scal[2]
    block = mine.shape[2]

    @pl.when(pl.program_id(0) < count)
    def _():
        placed = jnp.dot(norm[0], order[...], preferred_element_type=F32).astype(BF16)
        for start in range(0, dpre.shape[2], CHUNK):
            cols = slice(start, start + CHUNK)
            product[:, cols] = lax.dot_general(
                placed, dpre[0, :, cols], TN, preferred_element_type=F32
            )

    @pl.when(pl.program_id(0) >= count)
    def _():
        product[...] = jnp.zeros_like(product)

    for i in range(4):
        low = pl.multiple_of((core * 4 + i) * block, 8)
        mine[i, 0] = product[pl.ds(low, block), :].astype(BF16)
        low = pl.multiple_of(((1 - core) * 4 + i) * block, 8)
        theirs[i, 0] = product[pl.ds(low, block), :].astype(BF16)


def up_grad_call(scal, norms, dpres, order):
    slots, rows, width = norms.shape
    hidden_width = dpres.shape[2]
    block = width // 8
    shape = jax.ShapeDtypeStruct((4, slots, block, hidden_width), BF16)
    spec = pl.BlockSpec((4, 1, block, hidden_width), lambda j: (0, j, 0, 0))
    return pl.pallas_call(
        up_grad_kernel,
        grid=(slots,),
        out_shape=(shape, shape),
        in_specs=[
            SMEM,
            pl.BlockSpec((1, rows, width), lambda j: (j, 0, 0)),
            pl.BlockSpec((1, rows, hidden_width), lambda j: (j, 0, 0)),
            pl.BlockSpec((width, width), lambda j: (0, 0)),
        ],
        out_specs=(spec, spec),
        scratch_shapes=[pltpu.VMEM((width, hidden_width), F32)],
        compiler_params=pltpu.CompilerParams(vmem_limit_bytes=VMEM_LIMIT),
        cost_estimate=pl.CostEstimate(
            flops=2 * slots * rows * width * hidden_width,
            bytes_accessed=12_000_000,
            transcendentals=0,
        ),
        name="up_grad",
    )(scal, norms, dpres, order)


def down_grad_kernel(scal, hidden, out_grad, skip_in, first, order, mine, theirs, product, prod_skip):
    stage, count, core = scal[0], scal[1], scal[2]
    slot = pl.program_id(0)
    slots = pl.num_programs(0)
    block = mine.shape[2]

    @pl.when(slot < count)
    def _():
        for start in range(0, hidden.shape[2], CHUNK):
            cols = slice(start, start + CHUNK)
            product[cols, :] = lax.dot_general(
                hidden[0, :, cols], out_grad[0], TN, preferred_element_type=F32
            )

    @pl.when((slot >= count) & (slot < slots - 1))
    def _():
        product[...] = jnp.zeros_like(product)

    @pl.when(slot == slots - 1)
    def _():
        prod_skip[...] = jnp.zeros_like(prod_skip)

    @pl.when((slot == slots - 1) & (stage >= 2))
    def _():
        placed = jnp.dot(skip_in[...], order[...], preferred_element_type=F32).astype(BF16)
        prod_skip[...] = lax.dot_general(placed, first[...], TN, preferred_element_type=F32)

    @pl.when(slot < slots - 1)
    def _():
        for y in range(4):
            for x in range(4):
                low = pl.multiple_of((8 * y + 2 * x + core) * block, 8)
                mine[y, x] = product[pl.ds(low, block), :].astype(BF16)
                low = pl.multiple_of((8 * y + 2 * x + 1 - core) * block, 8)
                theirs[y, x] = product[pl.ds(low, block), :].astype(BF16)

    @pl.when(slot == slots - 1)
    def _():
        for y in range(4):
            for x in range(1, 4):
                mine[y, x] = jnp.zeros(mine.shape[2:], BF16)
                theirs[y, x] = jnp.zeros(mine.shape[2:], BF16)
            low = pl.multiple_of((core * 4 + y) * block, 8)
            mine[y, 0] = prod_skip[pl.ds(low, block), :].astype(BF16)
            low = pl.multiple_of(((1 - core) * 4 + y) * block, 8)
            theirs[y, 0] = prod_skip[pl.ds(low, block), :].astype(BF16)


def down_grad_call(scal, hiddens, outs, skips, firsts, order):
    slots, rows, hidden_width = hiddens.shape
    width = outs.shape[2]
    block = width // 8
    shape = jax.ShapeDtypeStruct((4, 4 * slots + 1, block, width), BF16)
    spec = pl.BlockSpec((4, 4, block, width), lambda j: (0, j, 0, 0))
    last = slots - 1
    return pl.pallas_call(
        down_grad_kernel,
        grid=(slots + 1,),
        out_shape=(shape, shape),
        in_specs=[
            SMEM,
            pl.BlockSpec((1, rows, hidden_width), lambda j: (jnp.minimum(j, last), 0, 0)),
            pl.BlockSpec((1, rows, width), lambda j: (jnp.minimum(j, last), 0, 0)),
            pl.BlockSpec((rows, width), lambda j: (0, 0)),
            pl.BlockSpec((rows, width), lambda j: (0, 0)),
            pl.BlockSpec((width, width), lambda j: (0, 0)),
        ],
        out_specs=(spec, spec),
        scratch_shapes=[pltpu.VMEM((hidden_width, width), F32), pltpu.VMEM((width, width), F32)],
        compiler_params=pltpu.CompilerParams(vmem_limit_bytes=VMEM_LIMIT),
        cost_estimate=pl.CostEstimate(
            flops=2 * slots * rows * width * hidden_width,
            bytes_accessed=12_000_000,
            transcendentals=0,
        ),
        name="down_grad",
    )(scal, hiddens, outs, skips, firsts, order)


def block_order(width, first, second):
    block = width // 32
    matrix = np.zeros((width, width), ml_dtypes.bfloat16)
    for y in range(4):
        for x in range(4):
            for core in range(2):
                where = {"x": x, "y": y}
                place = (core * 4 + where[first]) * 4 + where[second]
                source = 8 * y + 2 * x + core
                for r in range(block):
                    matrix[source * block + r, place * block + r] = 1
    return jnp.asarray(matrix)


def shifted(size, distance):
    return [(i, (i + distance) % size) for i in range(size)]


def scattered(pieces, axis, out_type):
    size = lax.axis_size(axis)
    index = lax.axis_index(axis)
    arrived = [
        lax.ppermute(pieces(lax.rem(index + d, size)), axis, shifted(size, d)) for d in (2, 1, 3)
    ]
    total = pieces(index).astype(F32)
    for value in arrived:
        total = total + value.astype(F32)
    return total.astype(out_type)


def take(value, index, dim):
    return lax.dynamic_index_in_dim(value, index, dim, keepdims=False)


def per_device(
    latents, cotangent, timesteps, layer_count, up_weight, down_weight, time_weight, skip_weight
):
    sections = lax.axis_size("pipe")
    stage = lax.axis_index("pipe")
    core = lax.axis_index("core")
    samples, rows, width = latents.shape
    up, down, skip_mat = up_weight[0], down_weight[0], skip_weight[0]
    slots, _, hidden_width = up.shape
    scal = jnp.stack([stage, layer_count[0], core, core]).astype(jnp.int32)
    condition = jax.nn.silu(embedding(timesteps, width // 2)).astype(BF16)
    modulation = jnp.einsum("mt,jtc->mjc", condition, time_weight[0], preferred_element_type=F32)

    ticks = samples + 2 * (sections - 1)
    empty = jnp.zeros((rows, width), BF16)
    moved = {}
    skips_moved = {}
    saved = None
    for tick in range(ticks):
        incoming = moved.get(tick - 2, empty)
        sent, saved = forward_call(
            tick,
            scal,
            modulation,
            latents,
            incoming,
            up,
            down,
            skip_mat,
            skips_moved.get(tick - 2 * (sections - 1)),
            saved,
        )
        pairs = [(z, z + 1) for z in range(sections - 1) if 0 <= tick - 2 * z < samples]
        if pairs:
            moved[tick] = lax.ppermute(sent, "pipe", pairs)
        if tick < samples:
            skips_moved[tick] = lax.ppermute(sent, "pipe", [(0, sections - 1)])
    states, pres, skips = saved

    moved = {}
    skips_moved = {}
    kept = None
    for tick in range(ticks):
        incoming = moved.get(tick - 2, empty)
        sent, sent_skip, kept = backward_call(
            tick,
            scal,
            modulation,
            cotangent,
            incoming,
            up,
            down,
            skip_mat,
            states,
            pres,
            skips_moved.get(tick - 2 * (sections - 1)),
            kept,
        )
        pairs = [
            (z, z - 1)
            for z in range(1, sections)
            if 0 <= tick - 2 * (sections - 1 - z) < samples
        ]
        if pairs:
            moved[tick] = lax.ppermute(sent, "pipe", pairs)
        if tick < samples:
            skips_moved[tick] = lax.ppermute(sent_skip, "pipe", [(sections - 1, 0)])
    norms, outs, hiddens, dpres, mod_grads, firsts = kept
    total_rows = samples * rows

    mine_down, theirs_down = down_grad_call(
        scal,
        hiddens.reshape(slots, total_rows, hidden_width),
        outs.reshape(slots, total_rows, width),
        skips.reshape(total_rows, width),
        firsts.reshape(total_rows, width),
        block_order(width, "y", "x"),
    )
    other_down = lax.ppermute(theirs_down, "core", [(0, 1), (1, 0)])
    mine_up, theirs_up = up_grad_call(
        scal,
        norms.reshape(slots, total_rows, width),
        dpres.reshape(slots, total_rows, hidden_width),
        block_order(width, "x", "y"),
    )
    other_up = lax.ppermute(theirs_up, "core", [(0, 1), (1, 0)])

    everywhere = ("y", "x", "core")
    small = jnp.concatenate(
        [condition, mod_grads.reshape(samples, slots * 2 * width).astype(BF16)], axis=1
    )
    gathered = lax.all_gather(small, everywhere, axis=0, tiled=True)

    def add(a, b):
        return (a.astype(F32) + b.astype(F32)).astype(BF16)

    sum_down = scattered(lambda i: add(take(mine_down, i, 0), take(other_down, i, 0)), "y", BF16)
    sum_up = scattered(lambda i: add(take(mine_up, i, 0), take(other_up, i, 0)), "x", BF16)
    block = width // 8
    down_part = sum_down[: 4 * slots].reshape(slots, 4, block, width)
    skip_part = sum_down[4 * slots].reshape(4, block // 4, width)
    up_part = sum_up.reshape(slots, 4, block // 4, hidden_width)

    def last_down(i):
        piece = take(down_part, i, 1).reshape(slots * block, width)
        return jnp.concatenate([piece, take(skip_part, i, 0)], axis=0)

    final_down = scattered(last_down, "x", F32)
    final_up = scattered(lambda i: take(up_part, i, 1), "y", F32)
    grad_down = final_down[: slots * block].reshape(slots, block, width)
    grad_skip = final_down[slots * block :]

    own = lax.axis_index(everywhere)
    own_rows = lax.dynamic_slice_in_dim(
        gathered[:, :width], own * (width // 32), width // 32, axis=1
    )
    grad_time = jnp.einsum(
        "bt,bc->tc", own_rows, gathered[:, width:], preferred_element_type=F32
    )
    grad_time = grad_time.reshape(width // 32, slots, 2 * width).transpose(1, 0, 2)
    return (final_up[None], grad_down[None], grad_time[None], grad_skip[None])


def solution(mesh):
    split = Mesh(
        mesh.devices.reshape(4, 4, 2, mesh.devices.shape[1]), ("y", "x", "core", "pipe")
    )
    dp = ("y", "x", "core")
    placed = (
        P(dp, None, None),
        P(dp, None, None),
        P(dp),
        P("pipe"),
        P("pipe", None, None, None),
        P("pipe", None, None, None),
        P("pipe", None, None, None),
        P("pipe", None, None),
    )
    return jax.shard_map(
        per_device,
        mesh=split,
        in_specs=placed,
        out_specs=(
            P("pipe", None, dp, None),
            P("pipe", None, dp, None),
            P("pipe", None, dp, None),
            P("pipe", dp, None),
        ),
        check_vma=False,
    )
```

```python
import functools
import math

import jax
import jax.numpy as jnp
import ml_dtypes
import numpy as np
from jax import lax
from jax.experimental import pallas as pl
from jax.experimental.pallas import tpu as pltpu
from jax.sharding import Mesh
from jax.sharding import PartitionSpec as P

EPSILON = 1e-06
BF16 = jnp.bfloat16
F32 = jnp.float32
CHUNK = 256
VMEM_LIMIT = 40 * 1024 * 1024
ANY = pl.BlockSpec(memory_space=pltpu.HBM)
SMEM = pl.BlockSpec(memory_space=pltpu.SMEM)
NT = (((1,), (1,)), ((), ()))
TN = (((0,), (0,)), ((), ()))


def embedding(timesteps, halfway):
    frequency = jnp.exp(-math.log(10000.0) * jnp.arange(halfway, dtype=F32) / halfway)
    angles = timesteps.astype(F32)[..., None] * frequency
    return jnp.concatenate([jnp.sin(angles), jnp.cos(angles)], axis=-1)


def nt_dot(left, right):
    return lax.dot_general(left, right, NT, preferred_element_type=F32)


def sigmoid(value):
    return 0.5 * jnp.tanh(0.5 * value) + 0.5


def copies_in(pairs, sems):
    return [pltpu.make_async_copy(src, dst, sems.at[i]) for i, (src, dst) in enumerate(pairs)]


def forward_kernel(tick, has_saved, has_skip, samples, slots, sections, width, *refs):
    refs = list(refs)
    scal, mod, latents, incoming, up, down, skip_weight = refs[:7]
    del refs[:7]
    skip_in = refs.pop(0) if has_skip else None
    if has_saved:
        del refs[:3]
    out, states, pres, skips = refs[:4]
    xv, sv, modv, upv, downv, skwv, statev, prev, acc, hidv, sems = refs[4:]
    stage, count = scal[0], scal[1]
    sample = tick - 2 * stage
    hidden_width = upv.shape[2]
    half = sections // 2

    @pl.when((sample >= 0) & (sample < samples))
    def _():
        copy_latents = pltpu.make_async_copy(latents.at[sample], xv, sems.at[0])
        copy_incoming = pltpu.make_async_copy(incoming, xv, sems.at[0])
        copy_mod = pltpu.make_async_copy(mod.at[sample], modv, sems.at[1])
        copy_skw = pltpu.make_async_copy(skip_weight, skwv, sems.at[2])
        copy_up = copies_in([(up.at[j], upv.at[j]) for j in range(slots)], sems.at[pl.ds(4, slots)])
        copy_down = copies_in(
            [(down.at[j], downv.at[j]) for j in range(slots)], sems.at[pl.ds(4 + slots, slots)]
        )
        save_state = copies_in(
            [(statev.at[j], states.at[sample, j]) for j in range(slots)],
            sems.at[pl.ds(4 + 2 * slots, slots)],
        )
        save_pre = copies_in(
            [(prev.at[j], pres.at[sample, j]) for j in range(slots)],
            sems.at[pl.ds(4 + 3 * slots, slots)],
        )
        save_skip = pltpu.make_async_copy(sv, skips.at[sample], sems.at[3])

        @pl.when(stage == 0)
        def _():
            copy_latents.start()

        @pl.when(stage != 0)
        def _():
            copy_incoming.start()

        copy_mod.start()
        decoder = stage >= half

        @pl.when(decoder)
        def _():
            copy_skw.start()

        for j in range(slots):

            @pl.when(j < count)
            def _():
                copy_up[j].start()
                copy_down[j].start()

        copy_incoming.wait()
        acc[...] = xv[...].astype(F32)

        @pl.when(decoder)
        def _():
            if has_skip:
                copy_skip = pltpu.make_async_copy(skip_in, sv, sems.at[3])

                @pl.when(stage == sections - 1)
                def _():
                    copy_skip.start()
                    copy_skip.wait()

                @pl.when(stage != sections - 1)
                def _():
                    sv[...] = xv[...]

            else:
                sv[...] = xv[...]
            save_skip.start()
            copy_skw.wait()
            acc[...] += jnp.dot(sv[...], skwv[...], preferred_element_type=F32)

        copy_mod.wait()
        for j in range(slots):

            @pl.when(j < count)
            def _():
                copy_up[j].wait()
                copy_down[j].wait()
                state = acc[...]
                statev[j] = state
                scaling = modv[j : j + 1, :width]
                offset = modv[j : j + 1, width:]
                inverse = lax.rsqrt(jnp.mean(state * state, axis=-1, keepdims=True) + EPSILON)
                normed = (state * inverse * (1.0 + scaling) + offset).astype(BF16)
                for start in range(0, hidden_width, CHUNK):
                    cols = slice(start, start + CHUNK)
                    pre = jnp.dot(normed, upv[j, :, cols], preferred_element_type=F32)
                    prev[j, :, cols] = pre.astype(BF16)
                    hidv[:, cols] = (pre * sigmoid(pre)).astype(BF16)
                acc[...] = state + nt_dot(hidv[...], downv[j])
                save_state[j].start()
                save_pre[j].start()

        xv[...] = acc[...].astype(BF16)
        save_out = pltpu.make_async_copy(xv, out, sems.at[0])
        save_out.start()
        for j in range(slots):

            @pl.when(j < count)
            def _():
                save_state[j].wait()
                save_pre[j].wait()

        @pl.when(decoder)
        def _():
            save_skip.wait()

        save_out.wait()


def forward_call(tick, scal, mod, latents, incoming, up, down, skip_weight, skip_in, saved):
    samples, rows, width = latents.shape
    slots, _, hidden_width = up.shape
    shapes = (
        jax.ShapeDtypeStruct((rows, width), BF16),
        jax.ShapeDtypeStruct((samples, slots, rows, width), F32),
        jax.ShapeDtypeStruct((samples, slots, rows, hidden_width), BF16),
        jax.ShapeDtypeStruct((samples, rows, width), BF16),
    )
    operands = [scal, mod, latents, incoming, up, down, skip_weight]
    if skip_in is not None:
        operands.append(skip_in)
    aliases = {}
    if saved is not None:
        aliases = {len(operands) + i: 1 + i for i in range(3)}
        operands += list(saved)
    out = pl.pallas_call(
        functools.partial(
            forward_kernel,
            tick,
            saved is not None,
            skip_in is not None,
            samples,
            slots,
            4,
            width,
        ),
        out_shape=shapes,
        in_specs=[SMEM] + [ANY] * (len(operands) - 1),
        out_specs=(ANY,) * 4,
        input_output_aliases=aliases,
        scratch_shapes=[
            pltpu.VMEM((rows, width), BF16),
            pltpu.VMEM((rows, width), BF16),
            pltpu.VMEM((slots, 2 * width), F32),
            pltpu.VMEM((slots, width, hidden_width), BF16),
            pltpu.VMEM((slots, width, hidden_width), BF16),
            pltpu.VMEM((width, width), BF16),
            pltpu.VMEM((slots, rows, width), F32),
            pltpu.VMEM((slots, rows, hidden_width), BF16),
            pltpu.VMEM((rows, width), F32),
            pltpu.VMEM((rows, hidden_width), BF16),
            pltpu.SemaphoreType.DMA((4 + 4 * slots,)),
        ],
        compiler_params=pltpu.CompilerParams(vmem_limit_bytes=VMEM_LIMIT),
        cost_estimate=pl.CostEstimate(
            flops=slots * rows * width * hidden_width * 4,
            bytes_accessed=8_000_000,
            transcendentals=0,
        ),
        name=f"section_forward_{tick}",
    )(*operands)
    return out[0], out[1:]


def backward_kernel(tick, has_saved, has_skip, samples, slots, sections, width, *refs):
    refs = list(refs)
    scal, mod, cotangent, incoming, up, down, skip_weight, states, pres = refs[:9]
    del refs[:9]
    skip_grad = refs.pop(0) if has_skip else None
    if has_saved:
        del refs[:6]
    out, out_skip, norms, outs, hiddens, dpres, mod_grads, firsts = refs[:8]
    gv, hv, modv, upv, downv, skwv, statev, prev, acc, nv, ov, hidv, dpv, mgv, fv, sems = refs[8:]
    stage, count = scal[0], scal[1]
    sample = tick - 2 * (sections - 1 - stage)
    hidden_width = upv.shape[2]
    half = sections // 2

    @pl.when((sample >= 0) & (sample < samples))
    def _():
        copy_cot = pltpu.make_async_copy(cotangent.at[sample], gv, sems.at[0])
        copy_incoming = pltpu.make_async_copy(incoming, gv, sems.at[0])
        copy_mod = pltpu.make_async_copy(mod.at[sample], modv, sems.at[1])
        copy_skw = pltpu.make_async_copy(skip_weight, skwv, sems.at[2])

        def group(index, pairs):
            return copies_in(pairs, sems.at[pl.ds(4 + index * slots, slots)])

        each = range(slots)
        copy_up = group(0, [(up.at[j], upv.at[j]) for j in each])
        copy_down = group(1, [(down.at[j], downv.at[j]) for j in each])
        copy_state = group(2, [(states.at[sample, j], statev.at[j]) for j in each])
        copy_pre = group(3, [(pres.at[sample, j], prev.at[j]) for j in each])
        save_norm = group(4, [(nv.at[j], norms.at[j, sample]) for j in each])
        save_out = group(5, [(ov.at[j], outs.at[j, sample]) for j in each])
        save_hid = group(6, [(hidv.at[j], hiddens.at[j, sample]) for j in each])
        save_dpre = group(7, [(dpv.at[j], dpres.at[j, sample]) for j in each])

        @pl.when(stage == sections - 1)
        def _():
            copy_cot.start()

        @pl.when(stage != sections - 1)
        def _():
            copy_incoming.start()

        if has_skip:
            copy_skip = pltpu.make_async_copy(skip_grad, hv, sems.at[3])

            @pl.when(stage == 0)
            def _():
                copy_skip.start()

        copy_mod.start()
        decoder = stage >= half
        for j in reversed(each):

            @pl.when(j < count)
            def _():
                copy_down[j].start()
                copy_pre[j].start()
                copy_up[j].start()
                copy_state[j].start()

        @pl.when(decoder)
        def _():
            copy_skw.start()

        copy_incoming.wait()
        if has_skip:

            @pl.when(stage == 0)
            def _():
                copy_skip.wait()
                acc[...] = (gv[...] + hv[...]).astype(F32)

            @pl.when(stage != 0)
            def _():
                acc[...] = gv[...].astype(F32)

        else:
            acc[...] = gv[...].astype(F32)
        copy_mod.wait()
        mgv[...] = jnp.zeros_like(mgv)
        for j in reversed(each):

            @pl.when(j < count)
            def _():
                copy_down[j].wait()
                copy_pre[j].wait()
                copy_up[j].wait()
                copy_state[j].wait()
                grad = acc[...]
                grad_b = grad.astype(BF16)
                ov[j] = grad_b
                for start in range(0, hidden_width, CHUNK):
                    cols = slice(start, start + CHUNK)
                    grad_hidden = jnp.dot(grad_b, downv[j, :, cols], preferred_element_type=F32)
                    pre = prev[j, :, cols].astype(F32)
                    gate = sigmoid(pre)
                    hidden = pre * gate
                    hidv[j, :, cols] = hidden.astype(BF16)
                    dpv[j, :, cols] = (
                        grad_hidden * (gate + hidden * (1.0 - gate))
                    ).astype(BF16)
                total = nt_dot(dpv[j], upv[j])
                state = statev[j]
                scaling = 1.0 + modv[j : j + 1, :width]
                offset = modv[j : j + 1, width:]
                inverse = lax.rsqrt(jnp.mean(state * state, axis=-1, keepdims=True) + EPSILON)
                unit = state * inverse
                nv[j] = (unit * scaling + offset).astype(BF16)
                grad_norm = total.astype(BF16).astype(F32)
                scaled = grad_norm * unit
                mgv[j : j + 1, :width] = jnp.sum(scaled, axis=0, keepdims=True)
                mgv[j : j + 1, width:] = jnp.sum(grad_norm, axis=0, keepdims=True)
                inner = jnp.mean(scaled * scaling, axis=-1, keepdims=True)
                acc[...] = grad + inverse * (grad_norm * scaling - unit * inner)
                save_out[j].start()
                save_hid[j].start()
                save_dpre[j].start()
                save_norm[j].start()

        save_mods = pltpu.make_async_copy(mgv, mod_grads.at[sample], sems.at[1])
        save_mods.start()
        first = acc[...].astype(BF16)
        fv[...] = first
        gv[...] = first
        save_first = pltpu.make_async_copy(fv, firsts.at[sample], sems.at[3])
        save_first.start()

        @pl.when(decoder)
        def _():
            copy_skw.wait()
            grad_skip = nt_dot(first, skwv[...]).astype(BF16)
            hv[...] = grad_skip

            @pl.when(stage == half)
            def _():
                gv[...] = first + grad_skip

        save_down = pltpu.make_async_copy(gv, out, sems.at[0])
        save_skip = pltpu.make_async_copy(hv, out_skip, sems.at[2])
        save_down.start()

        @pl.when(stage == sections - 1)
        def _():
            save_skip.start()
            save_skip.wait()

        for j in each:

            @pl.when(j < count)
            def _():
                save_norm[j].wait()
                save_out[j].wait()
                save_hid[j].wait()
                save_dpre[j].wait()

        save_first.wait()
        save_mods.wait()
        save_down.wait()


def backward_call(
    tick, scal, mod, cotangent, incoming, up, down, skip_weight, states, pres, skip_grad, saved
):
    samples, rows, width = cotangent.shape
    slots, _, hidden_width = up.shape
    narrow = (rows, width)
    wide = (rows, hidden_width)
    shapes = (
        jax.ShapeDtypeStruct(narrow, BF16),
        jax.ShapeDtypeStruct(narrow, BF16),
        jax.ShapeDtypeStruct((slots, samples, *narrow), BF16),
        jax.ShapeDtypeStruct((slots, samples, *narrow), BF16),
        jax.ShapeDtypeStruct((slots, samples, *wide), BF16),
        jax.ShapeDtypeStruct((slots, samples, *wide), BF16),
        jax.ShapeDtypeStruct((samples, slots, 2 * width), F32),
        jax.ShapeDtypeStruct((samples, *narrow), BF16),
    )
    operands = [scal, mod, cotangent, incoming, up, down, skip_weight, states, pres]
    if skip_grad is not None:
        operands.append(skip_grad)
    aliases = {}
    if saved is not None:
        aliases = {len(operands) + i: 2 + i for i in range(6)}
        operands += list(saved)
    out = pl.pallas_call(
        functools.partial(
            backward_kernel,
            tick,
            saved is not None,
            skip_grad is not None,
            samples,
            slots,
            4,
            width,
        ),
        out_shape=shapes,
        in_specs=[SMEM] + [ANY] * (len(operands) - 1),
        out_specs=(ANY,) * len(shapes),
        input_output_aliases=aliases,
        scratch_shapes=[
            pltpu.VMEM(narrow, BF16),
            pltpu.VMEM(narrow, BF16),
            pltpu.VMEM((slots, 2 * width), F32),
            pltpu.VMEM((slots, width, hidden_width), BF16),
            pltpu.VMEM((slots, width, hidden_width), BF16),
            pltpu.VMEM((width, width), BF16),
            pltpu.VMEM((slots, *narrow), F32),
            pltpu.VMEM((slots, *wide), BF16),
            pltpu.VMEM(narrow, F32),
            pltpu.VMEM((slots, *narrow), BF16),
            pltpu.VMEM((slots, *narrow), BF16),
            pltpu.VMEM((slots, *wide), BF16),
            pltpu.VMEM((slots, *wide), BF16),
            pltpu.VMEM((slots, 2 * width), F32),
            pltpu.VMEM(narrow, BF16),
            pltpu.SemaphoreType.DMA((4 + 8 * slots,)),
        ],
        compiler_params=pltpu.CompilerParams(vmem_limit_bytes=VMEM_LIMIT),
        cost_estimate=pl.CostEstimate(
            flops=slots * rows * width * hidden_width * 4,
            bytes_accessed=14_000_000,
            transcendentals=0,
        ),
        name=f"section_backward_{tick}",
    )(*operands)
    return out[0], out[1], out[2:]


def up_grad_kernel(scal, norm, dpre, order, condition, mod_grads, mine, theirs, product):
    count, core = scal[1], scal[2]
    slot = pl.program_id(0)
    slots = pl.num_programs(0) - 1
    block, lanes = mine.shape[2:]

    @pl.when(slot < count)
    def _():
        placed = jnp.dot(norm[0], order[...], preferred_element_type=F32).astype(BF16)
        for start in range(0, dpre.shape[2], CHUNK):
            cols = slice(start, start + CHUNK)
            product[:, cols] = lax.dot_general(
                placed, dpre[0, :, cols], TN, preferred_element_type=F32
            )

    @pl.when((slot >= count) & (slot < slots))
    def _():
        product[...] = jnp.zeros_like(product)

    @pl.when(slot == slots)
    def _():
        for half in range(2):
            product[:, half * lanes : (half + 1) * lanes] = time_product(condition, mod_grads, half)

    for i in range(4):
        for half in range(2):
            cols = slice(half * lanes, (half + 1) * lanes)
            low = pl.multiple_of((core * 4 + i) * block, 8)
            mine[i, half] = product[pl.ds(low, block), cols].astype(BF16)
            low = pl.multiple_of(((1 - core) * 4 + i) * block, 8)
            theirs[i, half] = product[pl.ds(low, block), cols].astype(BF16)


def time_product(condition, mod_grads, slot):
    total = condition[:, 0:1] * mod_grads[0, slot : slot + 1, :]
    for sample in range(1, mod_grads.shape[0]):
        total = total + (
            condition[:, sample : sample + 1] * mod_grads[sample, slot : slot + 1, :]
        )
    return total


def whole(shape):
    return pl.BlockSpec(shape, lambda j: (0,) * len(shape))


def up_grad_call(scal, norms, dpres, order, condition, mod_grads):
    slots, rows, width = norms.shape
    hidden_width = dpres.shape[2]
    block = width // 8
    last = slots - 1
    shape = jax.ShapeDtypeStruct((4, 2 * slots + 2, block, hidden_width // 2), BF16)
    spec = pl.BlockSpec((4, 2, block, hidden_width // 2), lambda j: (0, j, 0, 0))
    return pl.pallas_call(
        up_grad_kernel,
        grid=(slots + 1,),
        out_shape=(shape, shape),
        in_specs=[
            SMEM,
            pl.BlockSpec((1, rows, width), lambda j: (jnp.minimum(j, last), 0, 0)),
            pl.BlockSpec((1, rows, hidden_width), lambda j: (jnp.minimum(j, last), 0, 0)),
            whole((width, width)),
            whole(condition.shape),
            whole(mod_grads.shape),
        ],
        out_specs=(spec, spec),
        scratch_shapes=[pltpu.VMEM((width, hidden_width), F32)],
        compiler_params=pltpu.CompilerParams(vmem_limit_bytes=VMEM_LIMIT),
        cost_estimate=pl.CostEstimate(
            flops=2 * slots * rows * width * hidden_width,
            bytes_accessed=12_000_000,
            transcendentals=0,
        ),
        name="up_grad",
    )(scal, norms, dpres, order, condition, mod_grads)


def down_grad_kernel(
    scal,
    hidden,
    out_grad,
    skip_in,
    first,
    order,
    condition,
    mod_grads,
    mine,
    theirs,
    product,
    prod_time,
    prod_skip,
):
    stage, count, core = scal[0], scal[1], scal[2]
    slot = pl.program_id(0)
    slots = pl.num_programs(0) - 1
    block, lanes = mine.shape[2:]
    width = lanes // 2

    @pl.when(slot < count)
    def _():
        for start in range(0, hidden.shape[2], CHUNK):
            cols = slice(start, start + CHUNK)
            product[cols, :] = lax.dot_general(
                hidden[0, :, cols], out_grad[0], TN, preferred_element_type=F32
            )

    @pl.when((slot >= count) & (slot < slots))
    def _():
        product[...] = jnp.zeros_like(product)

    @pl.when(slot == slots)
    def _():
        prod_skip[...] = jnp.zeros_like(prod_skip)
        prod_time[...] = time_product(condition, mod_grads, 2)

    @pl.when((slot == slots) & (stage >= 2))
    def _():
        placed = jnp.dot(skip_in[...], order[...], preferred_element_type=F32).astype(BF16)
        prod_skip[:, :width] = lax.dot_general(placed, first[...], TN, preferred_element_type=F32)

    @pl.when(slot < slots)
    def _():
        for target, side in ((mine, core), (theirs, 1 - core)):
            for y in range(4):
                for pair in range(2):
                    low = pl.multiple_of((8 * y + 4 * pair + side) * block, 8)
                    high = pl.multiple_of((8 * y + 4 * pair + 2 + side) * block, 8)
                    target[y, pair] = jnp.concatenate(
                        [product[pl.ds(low, block), :], product[pl.ds(high, block), :]], axis=1
                    ).astype(BF16)

    @pl.when(slot == slots)
    def _():
        for target, side in ((mine, core), (theirs, 1 - core)):
            for y in range(4):
                low = pl.multiple_of((side * 4 + y) * block, 8)
                target[y, 0] = prod_time[pl.ds(low, block), :].astype(BF16)
                target[y, 1] = prod_skip[pl.ds(low, block), :].astype(BF16)


def down_grad_call(scal, hiddens, outs, skips, firsts, order, condition, mod_grads):
    slots, rows, hidden_width = hiddens.shape
    width = outs.shape[2]
    block = width // 8
    shape = jax.ShapeDtypeStruct((4, 2 * slots + 2, block, 2 * width), BF16)
    spec = pl.BlockSpec((4, 2, block, 2 * width), lambda j: (0, j, 0, 0))
    last = slots - 1
    return pl.pallas_call(
        down_grad_kernel,
        grid=(slots + 1,),
        out_shape=(shape, shape),
        in_specs=[
            SMEM,
            pl.BlockSpec((1, rows, hidden_width), lambda j: (jnp.minimum(j, last), 0, 0)),
            pl.BlockSpec((1, rows, width), lambda j: (jnp.minimum(j, last), 0, 0)),
            whole((rows, width)),
            whole((rows, width)),
            whole((width, width)),
            whole(condition.shape),
            whole(mod_grads.shape),
        ],
        out_specs=(spec, spec),
        scratch_shapes=[
            pltpu.VMEM((hidden_width, width), F32),
            pltpu.VMEM((width, 2 * width), F32),
            pltpu.VMEM((width, 2 * width), F32),
        ],
        compiler_params=pltpu.CompilerParams(vmem_limit_bytes=VMEM_LIMIT),
        cost_estimate=pl.CostEstimate(
            flops=2 * slots * rows * width * hidden_width,
            bytes_accessed=12_000_000,
            transcendentals=0,
        ),
        name="down_grad",
    )(scal, hiddens, outs, skips, firsts, order, condition, mod_grads)


def block_order(width, first, second):
    block = width // 32
    matrix = np.zeros((width, width), ml_dtypes.bfloat16)
    for y in range(4):
        for x in range(4):
            for core in range(2):
                where = {"x": x, "y": y}
                place = (core * 4 + where[first]) * 4 + where[second]
                source = 8 * y + 2 * x + core
                for r in range(block):
                    matrix[source * block + r, place * block + r] = 1
    return jnp.asarray(matrix)


def shifted(size, distance):
    return [(i, (i + distance) % size) for i in range(size)]


def scattered(pieces, axis, out_type):
    size = lax.axis_size(axis)
    index = lax.axis_index(axis)
    arrived = [
        lax.ppermute(pieces(lax.rem(index + d, size)), axis, shifted(size, d)) for d in (2, 1, 3)
    ]
    total = pieces(index).astype(F32)
    for value in arrived:
        total = total + value.astype(F32)
    return total.astype(out_type)


def halved(pieces, axis):
    size = lax.axis_size(axis)
    index = lax.axis_index(axis)
    own, ahead, across, behind = (pieces(lax.rem(index + d, size)) for d in (0, 1, 2, 3))
    cut = own.shape[0] // 2
    forward, backward = shifted(size, 1), shifted(size, size - 1)
    from_behind = lax.ppermute(jnp.concatenate([across[:cut], ahead[cut:]]), axis, forward)
    from_ahead = lax.ppermute(jnp.concatenate([across[cut:], behind[:cut]]), axis, backward)
    rest = own.shape[0] - cut
    passed_on = lax.ppermute(add(ahead[:cut], from_behind[:cut]), axis, forward)
    passed_back = lax.ppermute(add(behind[cut:], from_ahead[:rest]), axis, backward)
    low = add(own[:cut], from_ahead[rest:], passed_on)
    high = add(own[cut:], from_behind[cut:], passed_back)
    return jnp.concatenate([low, high])


def add(*terms):
    total = terms[0].astype(F32)
    for term in terms[1:]:
        total = total + term.astype(F32)
    return total.astype(BF16)


def take(value, index, dim):
    return lax.dynamic_index_in_dim(value, index, dim, keepdims=False)


def per_device(
    latents, cotangent, timesteps, layer_count, up_weight, down_weight, time_weight, skip_weight
):
    sections = lax.axis_size("pipe")
    stage = lax.axis_index("pipe")
    core = lax.axis_index("core")
    samples, rows, width = latents.shape
    up, down, skip_mat = up_weight[0], down_weight[0].swapaxes(1, 2), skip_weight[0]
    slots, _, hidden_width = up.shape
    scal = jnp.stack([stage, layer_count[0], core, core]).astype(jnp.int32)
    condition = jax.nn.silu(embedding(timesteps, width // 2)).astype(BF16)
    modulation = jnp.einsum("mt,jtc->mjc", condition, time_weight[0], preferred_element_type=F32)
    order_x = block_order(width, "x", "y")
    order_y = block_order(width, "y", "x")

    def columns(order):
        placed = lax.dot_general(order, condition, (((0,), (1,)), ((), ())))
        return placed.astype(F32)

    condition_x, condition_y = columns(order_x), columns(order_y)

    ticks = samples + 2 * (sections - 1)
    empty = jnp.zeros((rows, width), BF16)
    moved = {}
    skips_moved = {}
    saved = None
    for tick in range(ticks):
        incoming = moved.get(tick - 2, empty)
        sent, saved = forward_call(
            tick,
            scal,
            modulation,
            latents,
            incoming,
            up,
            down,
            skip_mat,
            skips_moved.get(tick - 2 * (sections - 1)),
            saved,
        )
        pairs = [(z, z + 1) for z in range(sections - 1) if 0 <= tick - 2 * z < samples]
        if pairs:
            moved[tick] = lax.ppermute(sent, "pipe", pairs)
        if tick < samples:
            skips_moved[tick] = lax.ppermute(sent, "pipe", [(0, sections - 1)])
    states, pres, skips = saved

    moved = {}
    skips_moved = {}
    kept = None
    for tick in range(ticks):
        incoming = moved.get(tick - 2, empty)
        sent, sent_skip, kept = backward_call(
            tick,
            scal,
            modulation,
            cotangent,
            incoming,
            up,
            down,
            skip_mat,
            states,
            pres,
            skips_moved.get(tick - 2 * (sections - 1)),
            kept,
        )
        pairs = [
            (z, z - 1)
            for z in range(1, sections)
            if 0 <= tick - 2 * (sections - 1 - z) < samples
        ]
        if pairs:
            moved[tick] = lax.ppermute(sent, "pipe", pairs)
        if tick < samples:
            skips_moved[tick] = lax.ppermute(sent_skip, "pipe", [(sections - 1, 0)])
    norms, outs, hiddens, dpres, mod_grads, firsts = kept
    total_rows = samples * rows

    mine_up, theirs_up = up_grad_call(
        scal,
        norms.reshape(slots, total_rows, width),
        dpres.reshape(slots, total_rows, hidden_width),
        order_x,
        condition_x,
        mod_grads,
    )
    other_up = lax.ppermute(theirs_up, "core", [(0, 1), (1, 0)])
    mine_down, theirs_down = down_grad_call(
        scal,
        hiddens.reshape(slots, total_rows, hidden_width),
        outs.reshape(slots, total_rows, width),
        skips.reshape(total_rows, width),
        firsts.reshape(total_rows, width),
        order_y,
        condition_y,
        mod_grads,
    )
    other_down = lax.ppermute(theirs_down, "core", [(0, 1), (1, 0)])

    sum_up = halved(lambda i: add(take(mine_up, i, 0), take(other_up, i, 0)), "x")
    sum_down = halved(lambda i: add(take(mine_down, i, 0), take(other_down, i, 0)), "y")
    block, part = width // 8, width // 32
    blocks = 2 * slots
    down_part = sum_down[:blocks].reshape(slots, 2, block, 2, width).transpose(1, 3, 0, 2, 4)
    down_part = down_part.reshape(4, slots * block, width)
    time_part = sum_down[blocks].reshape(4, part, 2, width).transpose(0, 2, 1, 3)
    skip_part = sum_down[blocks + 1, :, :width].reshape(4, part, width)
    down_part = jnp.concatenate(
        [down_part, time_part.reshape(4, 2 * part, width), skip_part], axis=1
    )
    up_part = sum_up.reshape(blocks + 2, 4, part, 2 * width)

    final_up = scattered(lambda i: take(up_part, i, 1), "y", F32)
    final_down = scattered(lambda i: take(down_part, i, 0), "x", F32)
    grad_up = final_up[:blocks].reshape(slots, 2, part, 2 * width).transpose(0, 2, 1, 3)
    grad_up = grad_up.reshape(slots, part, hidden_width)
    grad_down = final_down[: slots * block].reshape(slots, block, width)
    last_time = final_down[slots * block : slots * block + 2 * part].reshape(2, part, width)
    last_time = last_time.transpose(1, 0, 2).reshape(1, part, 2 * width)
    grad_time = jnp.concatenate([final_up[blocks:], last_time])
    grad_skip = final_down[slots * block + 2 * part :]
    return (grad_up[None], grad_down[None], grad_time[None], grad_skip[None])


def solution(mesh):
    split = Mesh(
        mesh.devices.reshape(4, 4, 2, mesh.devices.shape[1]), ("y", "x", "core", "pipe")
    )
    dp = ("y", "x", "core")
    placed = (
        P(dp, None, None),
        P(dp, None, None),
        P(dp),
        P("pipe"),
        P("pipe", None, None, None),
        P("pipe", None, None, None),
        P("pipe", None, None, None),
        P("pipe", None, None),
    )
    return jax.shard_map(
        per_device,
        mesh=split,
        in_specs=placed,
        out_specs=(
            P("pipe", None, dp, None),
            P("pipe", None, dp, None),
            P("pipe", None, dp, None),
            P("pipe", dp, None),
        ),
        check_vma=False,
    )
```

```python
import functools
import math

import jax
import jax.numpy as jnp
import ml_dtypes
import numpy as np
from jax import lax
from jax.experimental import pallas as pl
from jax.experimental.pallas import tpu as pltpu
from jax.sharding import Mesh
from jax.sharding import PartitionSpec as P

EPSILON = 1e-06
BF16 = jnp.bfloat16
F32 = jnp.float32
CHUNK = 256
SECTION_VMEM = 50 * 1024 * 1024
GRAD_VMEM = 56 * 1024 * 1024
ANY = pl.BlockSpec(memory_space=pl.ANY)
SMEM = pl.BlockSpec(memory_space=pltpu.SMEM)
NT = (((1,), (1,)), ((), ()))
TN = (((0,), (0,)), ((), ()))


def embedding(timesteps, halfway):
    frequency = jnp.exp(-math.log(10000.0) * jnp.arange(halfway, dtype=F32) / halfway)
    angles = timesteps.astype(F32)[..., None] * frequency
    return jnp.concatenate([jnp.sin(angles), jnp.cos(angles)], axis=-1)


def nt_dot(left, right):
    return lax.dot_general(left, right, NT, preferred_element_type=F32)


def sigmoid(value):
    return 0.5 * jnp.tanh(0.5 * value) + 0.5


def copies_in(pairs, sems):
    return [pltpu.make_async_copy(src, dst, sems.at[i]) for i, (src, dst) in enumerate(pairs)]


def forward_kernel(tick, has_saved, has_skip, samples, slots, sections, width, *refs):
    refs = list(refs)
    scal, mod, latents, incoming, up, down, skip_weight = refs[:7]
    del refs[:7]
    skip_in = refs.pop(0) if has_skip else None
    if has_saved:
        del refs[:3]
    out, states, pres, skips = refs[:4]
    xv, sv, modv, upv, downv, skwv, statev, prev, acc, hidv, sems = refs[4:]
    stage, count = scal[0], scal[1]
    sample = tick - 2 * stage
    hidden_width = upv.shape[2]
    half = sections // 2

    @pl.when((sample >= 0) & (sample < samples))
    def _():
        copy_latents = pltpu.make_async_copy(latents.at[sample], xv, sems.at[0])
        copy_incoming = pltpu.make_async_copy(incoming, xv, sems.at[0])
        copy_mod = pltpu.make_async_copy(mod.at[sample], modv, sems.at[1])
        copy_skw = pltpu.make_async_copy(skip_weight, skwv, sems.at[2])
        copy_up = copies_in([(up.at[j], upv.at[j]) for j in range(slots)], sems.at[pl.ds(4, slots)])
        copy_down = copies_in(
            [(down.at[j], downv.at[j]) for j in range(slots)], sems.at[pl.ds(4 + slots, slots)]
        )
        save_state = copies_in(
            [(statev.at[j], states.at[sample, j]) for j in range(slots)],
            sems.at[pl.ds(4 + 2 * slots, slots)],
        )
        save_pre = copies_in(
            [(prev.at[j], pres.at[sample, j]) for j in range(slots)],
            sems.at[pl.ds(4 + 3 * slots, slots)],
        )
        save_skip = pltpu.make_async_copy(sv, skips.at[sample], sems.at[3])

        @pl.when(stage == 0)
        def _():
            copy_latents.start()

        @pl.when(stage != 0)
        def _():
            copy_incoming.start()

        copy_mod.start()
        decoder = stage >= half

        @pl.when(decoder)
        def _():
            copy_skw.start()

        for j in range(slots):

            @pl.when(j < count)
            def _():
                copy_up[j].start()
                copy_down[j].start()

        copy_incoming.wait()
        acc[...] = xv[...].astype(F32)

        @pl.when(decoder)
        def _():
            if has_skip:
                copy_skip = pltpu.make_async_copy(skip_in, sv, sems.at[3])

                @pl.when(stage == sections - 1)
                def _():
                    copy_skip.start()
                    copy_skip.wait()

                @pl.when(stage != sections - 1)
                def _():
                    sv[...] = xv[...]

            else:
                sv[...] = xv[...]
            save_skip.start()
            copy_skw.wait()
            acc[...] += jnp.dot(sv[...], skwv[...], preferred_element_type=F32)

        copy_mod.wait()
        for j in range(slots):

            @pl.when(j < count)
            def _():
                copy_up[j].wait()
                copy_down[j].wait()
                state = acc[...]
                statev[j] = state
                scaling = modv[j : j + 1, :width]
                offset = modv[j : j + 1, width:]
                inverse = lax.rsqrt(jnp.mean(state * state, axis=-1, keepdims=True) + EPSILON)
                normed = (state * inverse * (1.0 + scaling) + offset).astype(BF16)
                for start in range(0, hidden_width, CHUNK):
                    cols = slice(start, start + CHUNK)
                    pre = jnp.dot(normed, upv[j, :, cols], preferred_element_type=F32)
                    prev[j, :, cols] = pre.astype(BF16)
                    hidv[:, cols] = (pre * sigmoid(pre)).astype(BF16)
                acc[...] = state + nt_dot(hidv[...], downv[j])
                save_state[j].start()
                save_pre[j].start()

        xv[...] = acc[...].astype(BF16)
        save_out = pltpu.make_async_copy(xv, out, sems.at[0])
        save_out.start()
        for j in range(slots):

            @pl.when(j < count)
            def _():
                save_state[j].wait()
                save_pre[j].wait()

        @pl.when(decoder)
        def _():
            save_skip.wait()

        save_out.wait()


def forward_call(tick, scal, mod, latents, incoming, up, down, skip_weight, skip_in, saved):
    samples, rows, width = latents.shape
    slots, _, hidden_width = up.shape
    shapes = (
        jax.ShapeDtypeStruct((rows, width), BF16),
        jax.ShapeDtypeStruct((samples, slots, rows, width), F32),
        jax.ShapeDtypeStruct((samples, slots, rows, hidden_width), BF16),
        jax.ShapeDtypeStruct((samples, rows, width), BF16),
    )
    operands = [scal, mod, latents, incoming, up, down, skip_weight]
    if skip_in is not None:
        operands.append(skip_in)
    aliases = {}
    if saved is not None:
        aliases = {len(operands) + i: 1 + i for i in range(3)}
        operands += list(saved)
    out = pl.pallas_call(
        functools.partial(
            forward_kernel,
            tick,
            saved is not None,
            skip_in is not None,
            samples,
            slots,
            4,
            width,
        ),
        out_shape=shapes,
        in_specs=[SMEM] + [ANY] * (len(operands) - 1),
        out_specs=(ANY,) * 4,
        input_output_aliases=aliases,
        scratch_shapes=[
            pltpu.VMEM((rows, width), BF16),
            pltpu.VMEM((rows, width), BF16),
            pltpu.VMEM((slots, 2 * width), F32),
            pltpu.VMEM((slots, width, hidden_width), BF16),
            pltpu.VMEM((slots, width, hidden_width), BF16),
            pltpu.VMEM((width, width), BF16),
            pltpu.VMEM((slots, rows, width), F32),
            pltpu.VMEM((slots, rows, hidden_width), BF16),
            pltpu.VMEM((rows, width), F32),
            pltpu.VMEM((rows, hidden_width), BF16),
            pltpu.SemaphoreType.DMA((4 + 4 * slots,)),
        ],
        compiler_params=pltpu.CompilerParams(vmem_limit_bytes=SECTION_VMEM),
        cost_estimate=pl.CostEstimate(
            flops=slots * rows * width * hidden_width * 4,
            bytes_accessed=8_000_000,
            transcendentals=0,
        ),
        name=f"section_forward_{tick}",
    )(*operands)
    return out[0], out[1:]


def backward_kernel(tick, has_saved, has_skip, samples, slots, sections, width, *refs):
    refs = list(refs)
    scal, mod, cotangent, incoming, up, down, skip_weight, states, pres = refs[:9]
    del refs[:9]
    skip_grad = refs.pop(0) if has_skip else None
    if has_saved:
        del refs[:6]
    out, out_skip, norms, outs, hiddens, dpres, mod_grads, firsts = refs[:8]
    gv, hv, modv, upv, downv, skwv, statev, prev, acc, nv, ov, hidv, dpv, mgv, fv, sems = refs[8:]
    stage, count = scal[0], scal[1]
    sample = tick - 2 * (sections - 1 - stage)
    hidden_width = upv.shape[2]
    half = sections // 2

    @pl.when((sample >= 0) & (sample < samples))
    def _():
        copy_cot = pltpu.make_async_copy(cotangent.at[sample], gv, sems.at[0])
        copy_incoming = pltpu.make_async_copy(incoming, gv, sems.at[0])
        copy_mod = pltpu.make_async_copy(mod.at[sample], modv, sems.at[1])
        copy_skw = pltpu.make_async_copy(skip_weight, skwv, sems.at[2])

        def group(index, pairs):
            return copies_in(pairs, sems.at[pl.ds(4 + index * slots, slots)])

        each = range(slots)
        copy_up = group(0, [(up.at[j], upv.at[j]) for j in each])
        copy_down = group(1, [(down.at[j], downv.at[j]) for j in each])
        copy_state = group(2, [(states.at[sample, j], statev.at[j]) for j in each])
        copy_pre = group(3, [(pres.at[sample, j], prev.at[j]) for j in each])
        save_norm = group(4, [(nv.at[j], norms.at[j, sample]) for j in each])
        save_out = group(5, [(ov.at[j], outs.at[j, sample]) for j in each])
        save_hid = group(6, [(hidv.at[j], hiddens.at[j, sample]) for j in each])
        save_dpre = group(7, [(dpv.at[j], dpres.at[j, sample]) for j in each])

        @pl.when(stage == sections - 1)
        def _():
            copy_cot.start()

        @pl.when(stage != sections - 1)
        def _():
            copy_incoming.start()

        if has_skip:
            copy_skip = pltpu.make_async_copy(skip_grad, hv, sems.at[3])

            @pl.when(stage == 0)
            def _():
                copy_skip.start()

        copy_mod.start()
        decoder = stage >= half
        for j in reversed(each):

            @pl.when(j < count)
            def _():
                copy_down[j].start()
                copy_pre[j].start()
                copy_up[j].start()
                copy_state[j].start()

        @pl.when(decoder)
        def _():
            copy_skw.start()

        copy_incoming.wait()
        if has_skip:

            @pl.when(stage == 0)
            def _():
                copy_skip.wait()
                acc[...] = (gv[...] + hv[...]).astype(F32)

            @pl.when(stage != 0)
            def _():
                acc[...] = gv[...].astype(F32)

        else:
            acc[...] = gv[...].astype(F32)
        copy_mod.wait()
        mgv[...] = jnp.zeros_like(mgv)
        for j in reversed(each):

            @pl.when(j < count)
            def _():
                copy_down[j].wait()
                copy_pre[j].wait()
                copy_up[j].wait()
                copy_state[j].wait()
                grad = acc[...]
                grad_b = grad.astype(BF16)
                ov[j] = grad_b
                for start in range(0, hidden_width, CHUNK):
                    cols = slice(start, start + CHUNK)
                    grad_hidden = jnp.dot(grad_b, downv[j, :, cols], preferred_element_type=F32)
                    pre = prev[j, :, cols].astype(F32)
                    gate = sigmoid(pre)
                    hidden = pre * gate
                    hidv[j, :, cols] = hidden.astype(BF16)
                    dpv[j, :, cols] = (
                        grad_hidden * (gate + hidden * (1.0 - gate))
                    ).astype(BF16)
                total = nt_dot(dpv[j], upv[j])
                state = statev[j]
                scaling = 1.0 + modv[j : j + 1, :width]
                offset = modv[j : j + 1, width:]
                inverse = lax.rsqrt(jnp.mean(state * state, axis=-1, keepdims=True) + EPSILON)
                unit = state * inverse
                nv[j] = (unit * scaling + offset).astype(BF16)
                grad_norm = total.astype(BF16).astype(F32)
                scaled = grad_norm * unit
                mgv[j : j + 1, :width] = jnp.sum(scaled, axis=0, keepdims=True)
                mgv[j : j + 1, width:] = jnp.sum(grad_norm, axis=0, keepdims=True)
                inner = jnp.mean(scaled * scaling, axis=-1, keepdims=True)
                acc[...] = grad + inverse * (grad_norm * scaling - unit * inner)
                save_out[j].start()
                save_hid[j].start()
                save_dpre[j].start()
                save_norm[j].start()

        save_mods = pltpu.make_async_copy(mgv, mod_grads.at[sample], sems.at[1])
        save_mods.start()
        first = acc[...].astype(BF16)
        fv[...] = first
        gv[...] = first
        save_first = pltpu.make_async_copy(fv, firsts.at[sample], sems.at[3])
        save_first.start()

        @pl.when(decoder)
        def _():
            copy_skw.wait()
            grad_skip = nt_dot(first, skwv[...]).astype(BF16)
            hv[...] = grad_skip

            @pl.when(stage == half)
            def _():
                gv[...] = first + grad_skip

        save_down = pltpu.make_async_copy(gv, out, sems.at[0])
        save_skip = pltpu.make_async_copy(hv, out_skip, sems.at[2])
        save_down.start()

        @pl.when(stage == sections - 1)
        def _():
            save_skip.start()
            save_skip.wait()

        for j in each:

            @pl.when(j < count)
            def _():
                save_norm[j].wait()
                save_out[j].wait()
                save_hid[j].wait()
                save_dpre[j].wait()

        save_first.wait()
        save_mods.wait()
        save_down.wait()


def backward_call(
    tick, scal, mod, cotangent, incoming, up, down, skip_weight, states, pres, skip_grad, saved
):
    samples, rows, width = cotangent.shape
    slots, _, hidden_width = up.shape
    narrow = (rows, width)
    wide = (rows, hidden_width)
    shapes = (
        jax.ShapeDtypeStruct(narrow, BF16),
        jax.ShapeDtypeStruct(narrow, BF16),
        jax.ShapeDtypeStruct((slots, samples, *narrow), BF16),
        jax.ShapeDtypeStruct((slots, samples, *narrow), BF16),
        jax.ShapeDtypeStruct((slots, samples, *wide), BF16),
        jax.ShapeDtypeStruct((slots, samples, *wide), BF16),
        jax.ShapeDtypeStruct((samples, slots, 2 * width), F32),
        jax.ShapeDtypeStruct((samples, *narrow), BF16),
    )
    operands = [scal, mod, cotangent, incoming, up, down, skip_weight, states, pres]
    if skip_grad is not None:
        operands.append(skip_grad)
    aliases = {}
    if saved is not None:
        aliases = {len(operands) + i: 2 + i for i in range(6)}
        operands += list(saved)
    out = pl.pallas_call(
        functools.partial(
            backward_kernel,
            tick,
            saved is not None,
            skip_grad is not None,
            samples,
            slots,
            4,
            width,
        ),
        out_shape=shapes,
        in_specs=[SMEM] + [ANY] * (len(operands) - 1),
        out_specs=(ANY,) * len(shapes),
        input_output_aliases=aliases,
        scratch_shapes=[
            pltpu.VMEM(narrow, BF16),
            pltpu.VMEM(narrow, BF16),
            pltpu.VMEM((slots, 2 * width), F32),
            pltpu.VMEM((slots, width, hidden_width), BF16),
            pltpu.VMEM((slots, width, hidden_width), BF16),
            pltpu.VMEM((width, width), BF16),
            pltpu.VMEM((slots, *narrow), F32),
            pltpu.VMEM((slots, *wide), BF16),
            pltpu.VMEM(narrow, F32),
            pltpu.VMEM((slots, *narrow), BF16),
            pltpu.VMEM((slots, *narrow), BF16),
            pltpu.VMEM((slots, *wide), BF16),
            pltpu.VMEM((slots, *wide), BF16),
            pltpu.VMEM((slots, 2 * width), F32),
            pltpu.VMEM(narrow, BF16),
            pltpu.SemaphoreType.DMA((4 + 8 * slots,)),
        ],
        compiler_params=pltpu.CompilerParams(vmem_limit_bytes=SECTION_VMEM),
        cost_estimate=pl.CostEstimate(
            flops=slots * rows * width * hidden_width * 4,
            bytes_accessed=14_000_000,
            transcendentals=0,
        ),
        name=f"section_backward_{tick}",
    )(*operands)
    return out[0], out[1], out[2:]


def up_grad_kernel(scal, norm, dpre, order, condition, mod_grads, mine, theirs, product):
    count, core = scal[1], scal[2]
    slot = pl.program_id(0)
    slots = pl.num_programs(0) - 1
    block, lanes = mine.shape[2:]

    @pl.when(slot < count)
    def _():
        placed = jnp.dot(norm[0], order[...], preferred_element_type=F32).astype(BF16)
        for start in range(0, dpre.shape[2], CHUNK):
            cols = slice(start, start + CHUNK)
            product[:, cols] = lax.dot_general(
                placed, dpre[0, :, cols], TN, preferred_element_type=F32
            )

    @pl.when((slot >= count) & (slot < slots))
    def _():
        product[...] = jnp.zeros_like(product)

    @pl.when(slot == slots)
    def _():
        for half in range(2):
            product[:, half * lanes : (half + 1) * lanes] = time_product(condition, mod_grads, half)

    for i in range(4):
        for half in range(2):
            cols = slice(half * lanes, (half + 1) * lanes)
            low = pl.multiple_of((core * 4 + i) * block, 8)
            mine[i, half] = product[pl.ds(low, block), cols].astype(BF16)
            low = pl.multiple_of(((1 - core) * 4 + i) * block, 8)
            theirs[i, half] = product[pl.ds(low, block), cols].astype(BF16)


def time_product(condition, mod_grads, slot):
    total = condition[:, 0:1] * mod_grads[0, slot : slot + 1, :]
    for sample in range(1, mod_grads.shape[0]):
        total = total + (
            condition[:, sample : sample + 1] * mod_grads[sample, slot : slot + 1, :]
        )
    return total


def whole(shape):
    return pl.BlockSpec(shape, lambda j: (0,) * len(shape))


def up_grad_call(scal, norms, dpres, order, condition, mod_grads):
    slots, rows, width = norms.shape
    hidden_width = dpres.shape[2]
    block = width // 8
    last = slots - 1
    shape = jax.ShapeDtypeStruct((4, 2 * slots + 2, block, hidden_width // 2), BF16)
    spec = pl.BlockSpec((4, 2, block, hidden_width // 2), lambda j: (0, j, 0, 0))
    return pl.pallas_call(
        up_grad_kernel,
        grid=(slots + 1,),
        out_shape=(shape, shape),
        in_specs=[
            SMEM,
            pl.BlockSpec((1, rows, width), lambda j: (jnp.minimum(j, last), 0, 0)),
            pl.BlockSpec((1, rows, hidden_width), lambda j: (jnp.minimum(j, last), 0, 0)),
            whole((width, width)),
            whole(condition.shape),
            whole(mod_grads.shape),
        ],
        out_specs=(spec, spec),
        scratch_shapes=[pltpu.VMEM((width, hidden_width), F32)],
        compiler_params=pltpu.CompilerParams(vmem_limit_bytes=GRAD_VMEM),
        cost_estimate=pl.CostEstimate(
            flops=2 * slots * rows * width * hidden_width,
            bytes_accessed=12_000_000,
            transcendentals=0,
        ),
        name="up_grad",
    )(scal, norms, dpres, order, condition, mod_grads)


def down_grad_kernel(
    scal,
    hidden,
    out_grad,
    skip_in,
    first,
    order,
    condition,
    mod_grads,
    mine,
    theirs,
    product,
    prod_time,
    prod_skip,
):
    stage, count, core = scal[0], scal[1], scal[2]
    slot = pl.program_id(0)
    slots = pl.num_programs(0) - 1
    block, lanes = mine.shape[2:]
    width = lanes // 2

    @pl.when(slot < count)
    def _():
        for start in range(0, hidden.shape[2], CHUNK):
            cols = slice(start, start + CHUNK)
            product[cols, :] = lax.dot_general(
                hidden[0, :, cols], out_grad[0], TN, preferred_element_type=F32
            )

    @pl.when((slot >= count) & (slot < slots))
    def _():
        product[...] = jnp.zeros_like(product)

    @pl.when(slot == slots)
    def _():
        prod_skip[...] = jnp.zeros_like(prod_skip)
        prod_time[...] = time_product(condition, mod_grads, 2)

    @pl.when((slot == slots) & (stage >= 2))
    def _():
        placed = jnp.dot(skip_in[...], order[...], preferred_element_type=F32).astype(BF16)
        prod_skip[:, :width] = lax.dot_general(placed, first[...], TN, preferred_element_type=F32)

    @pl.when(slot < slots)
    def _():
        for target, side in ((mine, core), (theirs, 1 - core)):
            for y in range(4):
                for pair in range(2):
                    low = pl.multiple_of((8 * y + 4 * pair + side) * block, 8)
                    high = pl.multiple_of((8 * y + 4 * pair + 2 + side) * block, 8)
                    target[y, pair] = jnp.concatenate(
                        [product[pl.ds(low, block), :], product[pl.ds(high, block), :]], axis=1
                    ).astype(BF16)

    @pl.when(slot == slots)
    def _():
        for target, side in ((mine, core), (theirs, 1 - core)):
            for y in range(4):
                low = pl.multiple_of((side * 4 + y) * block, 8)
                target[y, 0] = prod_time[pl.ds(low, block), :].astype(BF16)
                target[y, 1] = prod_skip[pl.ds(low, block), :].astype(BF16)


def down_grad_call(scal, hiddens, outs, skips, firsts, order, condition, mod_grads):
    slots, rows, hidden_width = hiddens.shape
    width = outs.shape[2]
    block = width // 8
    shape = jax.ShapeDtypeStruct((4, 2 * slots + 2, block, 2 * width), BF16)
    spec = pl.BlockSpec((4, 2, block, 2 * width), lambda j: (0, j, 0, 0))
    last = slots - 1
    return pl.pallas_call(
        down_grad_kernel,
        grid=(slots + 1,),
        out_shape=(shape, shape),
        in_specs=[
            SMEM,
            pl.BlockSpec((1, rows, hidden_width), lambda j: (jnp.minimum(j, last), 0, 0)),
            pl.BlockSpec((1, rows, width), lambda j: (jnp.minimum(j, last), 0, 0)),
            whole((rows, width)),
            whole((rows, width)),
            whole((width, width)),
            whole(condition.shape),
            whole(mod_grads.shape),
        ],
        out_specs=(spec, spec),
        scratch_shapes=[
            pltpu.VMEM((hidden_width, width), F32),
            pltpu.VMEM((width, 2 * width), F32),
            pltpu.VMEM((width, 2 * width), F32),
        ],
        compiler_params=pltpu.CompilerParams(vmem_limit_bytes=GRAD_VMEM),
        cost_estimate=pl.CostEstimate(
            flops=2 * slots * rows * width * hidden_width,
            bytes_accessed=12_000_000,
            transcendentals=0,
        ),
        name="down_grad",
    )(scal, hiddens, outs, skips, firsts, order, condition, mod_grads)


def block_order(width, first, second):
    block = width // 32
    matrix = np.zeros((width, width), ml_dtypes.bfloat16)
    for y in range(4):
        for x in range(4):
            for core in range(2):
                where = {"x": x, "y": y}
                place = (core * 4 + where[first]) * 4 + where[second]
                source = 8 * y + 2 * x + core
                for r in range(block):
                    matrix[source * block + r, place * block + r] = 1
    return jnp.asarray(matrix)


def shifted(size, distance):
    return [(i, (i + distance) % size) for i in range(size)]


def scattered(pieces, axis, out_type):
    size = lax.axis_size(axis)
    index = lax.axis_index(axis)
    arrived = [
        lax.ppermute(pieces(lax.rem(index + d, size)), axis, shifted(size, d)) for d in (2, 1, 3)
    ]
    total = pieces(index).astype(F32)
    for value in arrived:
        total = total + value.astype(F32)
    return total.astype(out_type)


def halved(pieces, axis):
    size = lax.axis_size(axis)
    index = lax.axis_index(axis)
    own, ahead, across, behind = (pieces(lax.rem(index + d, size)) for d in (0, 1, 2, 3))
    cut = own.shape[0] // 2
    forward, backward = shifted(size, 1), shifted(size, size - 1)
    from_behind = lax.ppermute(jnp.concatenate([across[:cut], ahead[cut:]]), axis, forward)
    from_ahead = lax.ppermute(jnp.concatenate([across[cut:], behind[:cut]]), axis, backward)
    rest = own.shape[0] - cut
    passed_on = lax.ppermute(add(ahead[:cut], from_behind[:cut]), axis, forward)
    passed_back = lax.ppermute(add(behind[cut:], from_ahead[:rest]), axis, backward)
    low = add(own[:cut], from_ahead[rest:], passed_on)
    high = add(own[cut:], from_behind[cut:], passed_back)
    return jnp.concatenate([low, high])


def add(*terms):
    total = terms[0].astype(F32)
    for term in terms[1:]:
        total = total + term.astype(F32)
    return total.astype(BF16)


def take(value, index, dim):
    return lax.dynamic_index_in_dim(value, index, dim, keepdims=False)


def per_device(
    latents, cotangent, timesteps, layer_count, up_weight, down_weight, time_weight, skip_weight
):
    sections = lax.axis_size("pipe")
    stage = lax.axis_index("pipe")
    core = lax.axis_index("core")
    samples, rows, width = latents.shape
    up, down, skip_mat = up_weight[0], down_weight[0].swapaxes(1, 2), skip_weight[0]
    slots, _, hidden_width = up.shape
    scal = jnp.stack([stage, layer_count[0], core, core]).astype(jnp.int32)
    condition = jax.nn.silu(embedding(timesteps, width // 2)).astype(BF16)
    modulation = jnp.einsum("mt,jtc->mjc", condition, time_weight[0], preferred_element_type=F32)
    order_x = block_order(width, "x", "y")
    order_y = block_order(width, "y", "x")

    def columns(order):
        placed = lax.dot_general(order, condition, (((0,), (1,)), ((), ())))
        return placed.astype(F32)

    condition_x, condition_y = columns(order_x), columns(order_y)

    ticks = samples + 2 * (sections - 1)
    empty = jnp.zeros((rows, width), BF16)
    moved = {}
    skips_moved = {}
    saved = None
    for tick in range(ticks):
        incoming = moved.get(tick - 2, empty)
        sent, saved = forward_call(
            tick,
            scal,
            modulation,
            latents,
            incoming,
            up,
            down,
            skip_mat,
            skips_moved.get(tick - 2 * (sections - 1)),
            saved,
        )
        pairs = [(z, z + 1) for z in range(sections - 1) if 0 <= tick - 2 * z < samples]
        if pairs:
            moved[tick] = lax.ppermute(sent, "pipe", pairs)
        if tick < samples:
            skips_moved[tick] = lax.ppermute(sent, "pipe", [(0, sections - 1)])
    states, pres, skips = saved

    moved = {}
    skips_moved = {}
    kept = None
    for tick in range(ticks):
        incoming = moved.get(tick - 2, empty)
        sent, sent_skip, kept = backward_call(
            tick,
            scal,
            modulation,
            cotangent,
            incoming,
            up,
            down,
            skip_mat,
            states,
            pres,
            skips_moved.get(tick - 2 * (sections - 1)),
            kept,
        )
        pairs = [
            (z, z - 1)
            for z in range(1, sections)
            if 0 <= tick - 2 * (sections - 1 - z) < samples
        ]
        if pairs:
            moved[tick] = lax.ppermute(sent, "pipe", pairs)
        if tick < samples:
            skips_moved[tick] = lax.ppermute(sent_skip, "pipe", [(sections - 1, 0)])
    norms, outs, hiddens, dpres, mod_grads, firsts = kept
    total_rows = samples * rows

    mine_up, theirs_up = up_grad_call(
        scal,
        norms.reshape(slots, total_rows, width),
        dpres.reshape(slots, total_rows, hidden_width),
        order_x,
        condition_x,
        mod_grads,
    )
    other_up = lax.ppermute(theirs_up, "core", [(0, 1), (1, 0)])
    mine_down, theirs_down = down_grad_call(
        scal,
        hiddens.reshape(slots, total_rows, hidden_width),
        outs.reshape(slots, total_rows, width),
        skips.reshape(total_rows, width),
        firsts.reshape(total_rows, width),
        order_y,
        condition_y,
        mod_grads,
    )
    other_down = lax.ppermute(theirs_down, "core", [(0, 1), (1, 0)])

    sum_up = halved(lambda i: add(take(mine_up, i, 0), take(other_up, i, 0)), "x")
    sum_down = halved(lambda i: add(take(mine_down, i, 0), take(other_down, i, 0)), "y")
    block, part = width // 8, width // 32
    blocks = 2 * slots
    down_part = sum_down[:blocks].reshape(slots, 2, block, 2, width).transpose(1, 3, 0, 2, 4)
    down_part = down_part.reshape(4, slots * block, width)
    time_part = sum_down[blocks].reshape(4, part, 2, width).transpose(0, 2, 1, 3)
    skip_part = sum_down[blocks + 1, :, :width].reshape(4, part, width)
    down_part = jnp.concatenate(
        [down_part, time_part.reshape(4, 2 * part, width), skip_part], axis=1
    )
    up_part = sum_up.reshape(blocks + 2, 4, part, 2 * width)

    final_up = scattered(lambda i: take(up_part, i, 1), "y", F32)
    final_down = scattered(lambda i: take(down_part, i, 0), "x", F32)
    grad_up = final_up[:blocks].reshape(slots, 2, part, 2 * width).transpose(0, 2, 1, 3)
    grad_up = grad_up.reshape(slots, part, hidden_width)
    grad_down = final_down[: slots * block].reshape(slots, block, width)
    last_time = final_down[slots * block : slots * block + 2 * part].reshape(2, part, width)
    last_time = last_time.transpose(1, 0, 2).reshape(1, part, 2 * width)
    grad_time = jnp.concatenate([final_up[blocks:], last_time])
    grad_skip = final_down[slots * block + 2 * part :]
    return (grad_up[None], grad_down[None], grad_time[None], grad_skip[None])


def solution(mesh):
    split = Mesh(
        mesh.devices.reshape(4, 4, 2, mesh.devices.shape[1]), ("y", "x", "core", "pipe")
    )
    dp = ("y", "x", "core")
    placed = (
        P(dp, None, None),
        P(dp, None, None),
        P(dp),
        P("pipe"),
        P("pipe", None, None, None),
        P("pipe", None, None, None),
        P("pipe", None, None, None),
        P("pipe", None, None),
    )
    return jax.shard_map(
        per_device,
        mesh=split,
        in_specs=placed,
        out_specs=(
            P("pipe", None, dp, None),
            P("pipe", None, dp, None),
            P("pipe", None, dp, None),
            P("pipe", dp, None),
        ),
        check_vma=False,
    )
```

```python
import functools
import math

import jax
import jax.numpy as jnp
import ml_dtypes
import numpy as np
from jax import lax
from jax.experimental import pallas as pl
from jax.experimental.pallas import tpu as pltpu
from jax.sharding import Mesh
from jax.sharding import PartitionSpec as P

EPSILON = 1e-06
BF16 = jnp.bfloat16
F32 = jnp.float32
CHUNK = 256
SECTION_VMEM = 53 * 1024 * 1024
GRAD_VMEM = 56 * 1024 * 1024
ANY = pl.BlockSpec(memory_space=pl.ANY)
SMEM = pl.BlockSpec(memory_space=pltpu.SMEM)
NT = (((1,), (1,)), ((), ()))
TN = (((0,), (0,)), ((), ()))


def embedding(timesteps, halfway):
    frequency = jnp.exp(-math.log(10000.0) * jnp.arange(halfway, dtype=F32) / halfway)
    angles = timesteps.astype(F32)[..., None] * frequency
    return jnp.concatenate([jnp.sin(angles), jnp.cos(angles)], axis=-1)


def nt_dot(left, right):
    return lax.dot_general(left, right, NT, preferred_element_type=F32)


def sigmoid(value):
    return 0.5 * jnp.tanh(0.5 * value) + 0.5


def forward_kernel(tick, has_saved, has_skip, samples, slots, sections, width, *refs):
    refs = list(refs)
    scal, mod, latents, incoming, up, down, skip_weight = refs[:7]
    del refs[:7]
    skip_in = refs.pop(0) if has_skip else None
    if has_saved:
        del refs[:3]
    out, states, pres, skips = refs[:4]
    xv, sv, modv, upv, downv, skwv, statev, prev, acc, hidv, sems = refs[4:]
    stage, count = scal[0], scal[1]
    sample = tick - 2 * stage
    hidden_width = upv.shape[2]
    half = sections // 2

    @pl.when((sample >= 0) & (sample < samples))
    def _():
        copy_latents = pltpu.make_async_copy(latents.at[sample], xv, sems.at[0])
        copy_incoming = pltpu.make_async_copy(incoming, xv, sems.at[0])
        copy_mod = pltpu.make_async_copy(mod.at[sample], modv, sems.at[1])
        copy_skw = pltpu.make_async_copy(skip_weight, skwv, sems.at[2])

        def copy_up(j):
            return pltpu.make_async_copy(up.at[j], upv.at[j], sems.at[4 + j])

        def copy_down(j):
            return pltpu.make_async_copy(down.at[j], downv.at[j], sems.at[4 + slots + j])

        def save_state(j):
            return pltpu.make_async_copy(
                statev.at[j], states.at[sample, j], sems.at[4 + 2 * slots + j]
            )

        def save_pre(j):
            return pltpu.make_async_copy(prev.at[j], pres.at[sample, j], sems.at[4 + 3 * slots + j])

        save_skip = pltpu.make_async_copy(sv, skips.at[sample], sems.at[3])

        @pl.when(stage == 0)
        def _():
            copy_latents.start()

        @pl.when(stage != 0)
        def _():
            copy_incoming.start()

        copy_mod.start()
        decoder = stage >= half

        @pl.when(decoder)
        def _():
            copy_skw.start()

        @pl.loop(0, count)
        def _(j):
            copy_up(j).start()
            copy_down(j).start()

        copy_incoming.wait()
        acc[...] = xv[...].astype(F32)

        @pl.when(decoder)
        def _():
            if has_skip:
                copy_skip = pltpu.make_async_copy(skip_in, sv, sems.at[3])

                @pl.when(stage == sections - 1)
                def _():
                    copy_skip.start()
                    copy_skip.wait()

                @pl.when(stage != sections - 1)
                def _():
                    sv[...] = xv[...]

            else:
                sv[...] = xv[...]
            save_skip.start()
            copy_skw.wait()
            acc[...] += jnp.dot(sv[...], skwv[...], preferred_element_type=F32)

        copy_mod.wait()

        @pl.loop(0, count)
        def _(j):
            copy_up(j).wait()
            copy_down(j).wait()
            state = acc[...]
            statev[j] = state
            scaling = modv[pl.ds(j, 1), :width]
            offset = modv[pl.ds(j, 1), width:]
            inverse = lax.rsqrt(jnp.mean(state * state, axis=-1, keepdims=True) + EPSILON)
            normed = (state * inverse * (1.0 + scaling) + offset).astype(BF16)
            for start in range(0, hidden_width, CHUNK):
                cols = slice(start, start + CHUNK)
                pre = jnp.dot(normed, upv[j, :, cols], preferred_element_type=F32)
                prev[j, :, cols] = pre.astype(BF16)
                hidv[:, cols] = (pre * sigmoid(pre)).astype(BF16)
            acc[...] = state + nt_dot(hidv[...], downv[j])
            save_state(j).start()
            save_pre(j).start()

        xv[...] = acc[...].astype(BF16)
        save_out = pltpu.make_async_copy(xv, out, sems.at[0])
        save_out.start()

        @pl.loop(0, count)
        def _(j):
            save_state(j).wait()
            save_pre(j).wait()

        @pl.when(decoder)
        def _():
            save_skip.wait()

        save_out.wait()


def forward_call(tick, scal, mod, latents, incoming, up, down, skip_weight, skip_in, saved):
    samples, rows, width = latents.shape
    slots, _, hidden_width = up.shape
    shapes = (
        jax.ShapeDtypeStruct((rows, width), BF16),
        jax.ShapeDtypeStruct((samples, slots, rows, width), F32),
        jax.ShapeDtypeStruct((samples, slots, rows, hidden_width), BF16),
        jax.ShapeDtypeStruct((samples, rows, width), BF16),
    )
    operands = [scal, mod, latents, incoming, up, down, skip_weight]
    if skip_in is not None:
        operands.append(skip_in)
    aliases = {}
    if saved is not None:
        aliases = {len(operands) + i: 1 + i for i in range(3)}
        operands += list(saved)
    out = pl.pallas_call(
        functools.partial(
            forward_kernel,
            tick,
            saved is not None,
            skip_in is not None,
            samples,
            slots,
            4,
            width,
        ),
        out_shape=shapes,
        in_specs=[SMEM] + [ANY] * (len(operands) - 1),
        out_specs=(ANY,) * 4,
        input_output_aliases=aliases,
        scratch_shapes=[
            pltpu.VMEM((rows, width), BF16),
            pltpu.VMEM((rows, width), BF16),
            pltpu.VMEM((slots, 2 * width), F32),
            pltpu.VMEM((slots, width, hidden_width), BF16),
            pltpu.VMEM((slots, width, hidden_width), BF16),
            pltpu.VMEM((width, width), BF16),
            pltpu.VMEM((slots, rows, width), F32),
            pltpu.VMEM((slots, rows, hidden_width), BF16),
            pltpu.VMEM((rows, width), F32),
            pltpu.VMEM((rows, hidden_width), BF16),
            pltpu.SemaphoreType.DMA((4 + 4 * slots,)),
        ],
        compiler_params=pltpu.CompilerParams(vmem_limit_bytes=SECTION_VMEM),
        cost_estimate=pl.CostEstimate(
            flops=slots * rows * width * hidden_width * 4,
            bytes_accessed=8_000_000,
            transcendentals=0,
        ),
        name=f"section_forward_{tick}",
    )(*operands)
    return out[0], out[1:]


def backward_kernel(tick, has_saved, has_skip, samples, slots, sections, width, *refs):
    refs = list(refs)
    scal, mod, cotangent, incoming, up, down, skip_weight, states, pres = refs[:9]
    del refs[:9]
    skip_grad = refs.pop(0) if has_skip else None
    if has_saved:
        del refs[:6]
    out, out_skip, norms, outs, hiddens, dpres, mod_grads, firsts = refs[:8]
    gv, hv, modv, upv, downv, skwv, statev, prev, acc, nv, ov, hidv, dpv, mgv, fv, sems = refs[8:]
    stage, count = scal[0], scal[1]
    sample = tick - 2 * (sections - 1 - stage)
    hidden_width = upv.shape[2]
    half = sections // 2

    @pl.when((sample >= 0) & (sample < samples))
    def _():
        copy_cot = pltpu.make_async_copy(cotangent.at[sample], gv, sems.at[0])
        copy_incoming = pltpu.make_async_copy(incoming, gv, sems.at[0])
        copy_mod = pltpu.make_async_copy(mod.at[sample], modv, sems.at[1])
        copy_skw = pltpu.make_async_copy(skip_weight, skwv, sems.at[2])


        def copy(group, j, source, target):
            return pltpu.make_async_copy(source, target, sems.at[4 + group * slots + j])

        def loads(j):
            return (
                copy(0, j, down.at[j], downv.at[j]),
                copy(1, j, pres.at[sample, j], prev.at[j]),
                copy(2, j, up.at[j], upv.at[j]),
                copy(3, j, states.at[sample, j], statev.at[j]),
            )

        def saves(j):
            return (
                copy(4, j, nv.at[j], norms.at[j, sample]),
                copy(5, j, ov.at[j], outs.at[j, sample]),
                copy(6, j, hidv.at[j], hiddens.at[j, sample]),
                copy(7, j, dpv.at[j], dpres.at[j, sample]),
            )

        @pl.when(stage == sections - 1)
        def _():
            copy_cot.start()

        @pl.when(stage != sections - 1)
        def _():
            copy_incoming.start()

        if has_skip:
            copy_skip = pltpu.make_async_copy(skip_grad, hv, sems.at[3])

            @pl.when(stage == 0)
            def _():
                copy_skip.start()

        copy_mod.start()
        decoder = stage >= half

        @pl.loop(0, count)
        def _(i):
            for load in loads(count - 1 - i):
                load.start()

        @pl.when(decoder)
        def _():
            copy_skw.start()

        copy_incoming.wait()
        if has_skip:

            @pl.when(stage == 0)
            def _():
                copy_skip.wait()
                acc[...] = (gv[...] + hv[...]).astype(F32)

            @pl.when(stage != 0)
            def _():
                acc[...] = gv[...].astype(F32)

        else:
            acc[...] = gv[...].astype(F32)
        copy_mod.wait()
        mgv[...] = jnp.zeros_like(mgv)

        @pl.loop(0, count)
        def _(i):
            j = count - 1 - i
            for load in loads(j):
                load.wait()
            grad = acc[...]
            grad_b = grad.astype(BF16)
            ov[j] = grad_b
            for start in range(0, hidden_width, CHUNK):
                cols = slice(start, start + CHUNK)
                grad_hidden = jnp.dot(grad_b, downv[j, :, cols], preferred_element_type=F32)
                pre = prev[j, :, cols].astype(F32)
                gate = sigmoid(pre)
                hidden = pre * gate
                hidv[j, :, cols] = hidden.astype(BF16)
                dpv[j, :, cols] = (grad_hidden * (gate + hidden * (1.0 - gate))).astype(BF16)
            total = nt_dot(dpv[j], upv[j])
            state = statev[j]
            scaling = 1.0 + modv[pl.ds(j, 1), :width]
            offset = modv[pl.ds(j, 1), width:]
            inverse = lax.rsqrt(jnp.mean(state * state, axis=-1, keepdims=True) + EPSILON)
            unit = state * inverse
            nv[j] = (unit * scaling + offset).astype(BF16)
            grad_norm = total.astype(BF16).astype(F32)
            scaled = grad_norm * unit
            mgv[pl.ds(j, 1), :width] = jnp.sum(scaled, axis=0, keepdims=True)
            mgv[pl.ds(j, 1), width:] = jnp.sum(grad_norm, axis=0, keepdims=True)
            inner = jnp.mean(scaled * scaling, axis=-1, keepdims=True)
            acc[...] = grad + inverse * (grad_norm * scaling - unit * inner)
            for save in saves(j):
                save.start()

        save_mods = pltpu.make_async_copy(mgv, mod_grads.at[sample], sems.at[1])
        save_mods.start()
        first = acc[...].astype(BF16)
        fv[...] = first
        gv[...] = first
        save_first = pltpu.make_async_copy(fv, firsts.at[sample], sems.at[3])
        save_first.start()

        @pl.when(decoder)
        def _():
            copy_skw.wait()
            grad_skip = nt_dot(first, skwv[...]).astype(BF16)
            hv[...] = grad_skip

            @pl.when(stage == half)
            def _():
                gv[...] = first + grad_skip

        save_down = pltpu.make_async_copy(gv, out, sems.at[0])
        save_skip = pltpu.make_async_copy(hv, out_skip, sems.at[2])
        save_down.start()

        @pl.when(stage == sections - 1)
        def _():
            save_skip.start()
            save_skip.wait()

        @pl.loop(0, count)
        def _(j):
            for save in saves(j):
                save.wait()

        save_first.wait()
        save_mods.wait()
        save_down.wait()


def backward_call(
    tick, scal, mod, cotangent, incoming, up, down, skip_weight, states, pres, skip_grad, saved
):
    samples, rows, width = cotangent.shape
    slots, _, hidden_width = up.shape
    narrow = (rows, width)
    wide = (rows, hidden_width)
    shapes = (
        jax.ShapeDtypeStruct(narrow, BF16),
        jax.ShapeDtypeStruct(narrow, BF16),
        jax.ShapeDtypeStruct((slots, samples, *narrow), BF16),
        jax.ShapeDtypeStruct((slots, samples, *narrow), BF16),
        jax.ShapeDtypeStruct((slots, samples, *wide), BF16),
        jax.ShapeDtypeStruct((slots, samples, *wide), BF16),
        jax.ShapeDtypeStruct((samples, slots, 2 * width), F32),
        jax.ShapeDtypeStruct((samples, *narrow), BF16),
    )
    operands = [scal, mod, cotangent, incoming, up, down, skip_weight, states, pres]
    if skip_grad is not None:
        operands.append(skip_grad)
    aliases = {}
    if saved is not None:
        aliases = {len(operands) + i: 2 + i for i in range(6)}
        operands += list(saved)
    out = pl.pallas_call(
        functools.partial(
            backward_kernel,
            tick,
            saved is not None,
            skip_grad is not None,
            samples,
            slots,
            4,
            width,
        ),
        out_shape=shapes,
        in_specs=[SMEM] + [ANY] * (len(operands) - 1),
        out_specs=(ANY,) * len(shapes),
        input_output_aliases=aliases,
        scratch_shapes=[
            pltpu.VMEM(narrow, BF16),
            pltpu.VMEM(narrow, BF16),
            pltpu.VMEM((slots, 2 * width), F32),
            pltpu.VMEM((slots, width, hidden_width), BF16),
            pltpu.VMEM((slots, width, hidden_width), BF16),
            pltpu.VMEM((width, width), BF16),
            pltpu.VMEM((slots, *narrow), F32),
            pltpu.VMEM((slots, *wide), BF16),
            pltpu.VMEM(narrow, F32),
            pltpu.VMEM((slots, *narrow), BF16),
            pltpu.VMEM((slots, *narrow), BF16),
            pltpu.VMEM((slots, *wide), BF16),
            pltpu.VMEM((slots, *wide), BF16),
            pltpu.VMEM((slots, 2 * width), F32),
            pltpu.VMEM(narrow, BF16),
            pltpu.SemaphoreType.DMA((4 + 8 * slots,)),
        ],
        compiler_params=pltpu.CompilerParams(vmem_limit_bytes=SECTION_VMEM),
        cost_estimate=pl.CostEstimate(
            flops=slots * rows * width * hidden_width * 4,
            bytes_accessed=14_000_000,
            transcendentals=0,
        ),
        name=f"section_backward_{tick}",
    )(*operands)
    return out[0], out[1], out[2:]


def up_grad_kernel(scal, norm, dpre, order, condition, mod_grads, mine, theirs, product):
    count, core = scal[1], scal[2]
    slot = pl.program_id(0)
    slots = pl.num_programs(0) - 1
    block, lanes = mine.shape[2:]

    @pl.when(slot < count)
    def _():
        placed = jnp.dot(norm[0], order[...], preferred_element_type=F32).astype(BF16)
        for start in range(0, dpre.shape[2], CHUNK):
            cols = slice(start, start + CHUNK)
            product[:, cols] = lax.dot_general(
                placed, dpre[0, :, cols], TN, preferred_element_type=F32
            )

    @pl.when((slot >= count) & (slot < slots))
    def _():
        product[...] = jnp.zeros_like(product)

    @pl.when(slot == slots)
    def _():
        for half in range(2):
            product[:, half * lanes : (half + 1) * lanes] = time_product(condition, mod_grads, half)

    for i in range(4):
        for half in range(2):
            cols = slice(half * lanes, (half + 1) * lanes)
            low = pl.multiple_of((core * 4 + i) * block, 8)
            mine[i, half] = product[pl.ds(low, block), cols].astype(BF16)
            low = pl.multiple_of(((1 - core) * 4 + i) * block, 8)
            theirs[i, half] = product[pl.ds(low, block), cols].astype(BF16)


def time_product(condition, mod_grads, slot):
    total = condition[:, 0:1] * mod_grads[0, slot : slot + 1, :]
    for sample in range(1, mod_grads.shape[0]):
        total = total + (
            condition[:, sample : sample + 1] * mod_grads[sample, slot : slot + 1, :]
        )
    return total


def whole(shape):
    return pl.BlockSpec(shape, lambda j: (0,) * len(shape))


def up_grad_call(scal, norms, dpres, order, condition, mod_grads):
    slots, rows, width = norms.shape
    hidden_width = dpres.shape[2]
    block = width // 8
    last = slots - 1
    shape = jax.ShapeDtypeStruct((4, 2 * slots + 2, block, hidden_width // 2), BF16)
    spec = pl.BlockSpec((4, 2, block, hidden_width // 2), lambda j: (0, j, 0, 0))
    return pl.pallas_call(
        up_grad_kernel,
        grid=(slots + 1,),
        out_shape=(shape, shape),
        in_specs=[
            SMEM,
            pl.BlockSpec((1, rows, width), lambda j: (jnp.minimum(j, last), 0, 0)),
            pl.BlockSpec((1, rows, hidden_width), lambda j: (jnp.minimum(j, last), 0, 0)),
            whole((width, width)),
            whole(condition.shape),
            whole(mod_grads.shape),
        ],
        out_specs=(spec, spec),
        scratch_shapes=[pltpu.VMEM((width, hidden_width), F32)],
        compiler_params=pltpu.CompilerParams(vmem_limit_bytes=GRAD_VMEM),
        cost_estimate=pl.CostEstimate(
            flops=2 * slots * rows * width * hidden_width,
            bytes_accessed=12_000_000,
            transcendentals=0,
        ),
        name="up_grad",
    )(scal, norms, dpres, order, condition, mod_grads)


def down_grad_kernel(
    scal,
    hidden,
    out_grad,
    skip_in,
    first,
    order,
    condition,
    mod_grads,
    mine,
    theirs,
    product,
    prod_time,
    prod_skip,
):
    stage, count, core = scal[0], scal[1], scal[2]
    slot = pl.program_id(0)
    slots = pl.num_programs(0) - 1
    block, lanes = mine.shape[2:]
    width = lanes // 2

    @pl.when(slot < count)
    def _():
        for start in range(0, hidden.shape[2], CHUNK):
            cols = slice(start, start + CHUNK)
            product[cols, :] = lax.dot_general(
                hidden[0, :, cols], out_grad[0], TN, preferred_element_type=F32
            )

    @pl.when((slot >= count) & (slot < slots))
    def _():
        product[...] = jnp.zeros_like(product)

    @pl.when(slot == slots)
    def _():
        prod_skip[...] = jnp.zeros_like(prod_skip)
        prod_time[...] = time_product(condition, mod_grads, 2)

    @pl.when((slot == slots) & (stage >= 2))
    def _():
        placed = jnp.dot(skip_in[...], order[...], preferred_element_type=F32).astype(BF16)
        prod_skip[:, :width] = lax.dot_general(placed, first[...], TN, preferred_element_type=F32)

    @pl.when(slot < slots)
    def _():
        for target, side in ((mine, core), (theirs, 1 - core)):
            for y in range(4):
                for pair in range(2):
                    low = pl.multiple_of((8 * y + 4 * pair + side) * block, 8)
                    high = pl.multiple_of((8 * y + 4 * pair + 2 + side) * block, 8)
                    target[y, pair] = jnp.concatenate(
                        [product[pl.ds(low, block), :], product[pl.ds(high, block), :]], axis=1
                    ).astype(BF16)

    @pl.when(slot == slots)
    def _():
        for target, side in ((mine, core), (theirs, 1 - core)):
            for y in range(4):
                low = pl.multiple_of((side * 4 + y) * block, 8)
                target[y, 0] = prod_time[pl.ds(low, block), :].astype(BF16)
                target[y, 1] = prod_skip[pl.ds(low, block), :].astype(BF16)


def down_grad_call(scal, hiddens, outs, skips, firsts, order, condition, mod_grads):
    slots, rows, hidden_width = hiddens.shape
    width = outs.shape[2]
    block = width // 8
    shape = jax.ShapeDtypeStruct((4, 2 * slots + 2, block, 2 * width), BF16)
    spec = pl.BlockSpec((4, 2, block, 2 * width), lambda j: (0, j, 0, 0))
    last = slots - 1
    return pl.pallas_call(
        down_grad_kernel,
        grid=(slots + 1,),
        out_shape=(shape, shape),
        in_specs=[
            SMEM,
            pl.BlockSpec((1, rows, hidden_width), lambda j: (jnp.minimum(j, last), 0, 0)),
            pl.BlockSpec((1, rows, width), lambda j: (jnp.minimum(j, last), 0, 0)),
            whole((rows, width)),
            whole((rows, width)),
            whole((width, width)),
            whole(condition.shape),
            whole(mod_grads.shape),
        ],
        out_specs=(spec, spec),
        scratch_shapes=[
            pltpu.VMEM((hidden_width, width), F32),
            pltpu.VMEM((width, 2 * width), F32),
            pltpu.VMEM((width, 2 * width), F32),
        ],
        compiler_params=pltpu.CompilerParams(vmem_limit_bytes=GRAD_VMEM),
        cost_estimate=pl.CostEstimate(
            flops=2 * slots * rows * width * hidden_width,
            bytes_accessed=12_000_000,
            transcendentals=0,
        ),
        name="down_grad",
    )(scal, hiddens, outs, skips, firsts, order, condition, mod_grads)


def block_order(width, first, second):
    block = width // 32
    matrix = np.zeros((width, width), ml_dtypes.bfloat16)
    for y in range(4):
        for x in range(4):
            for core in range(2):
                where = {"x": x, "y": y}
                place = (core * 4 + where[first]) * 4 + where[second]
                source = 8 * y + 2 * x + core
                for r in range(block):
                    matrix[source * block + r, place * block + r] = 1
    return jnp.asarray(matrix)


def shifted(size, distance):
    return [(i, (i + distance) % size) for i in range(size)]


def scattered(pieces, axis, out_type):
    size = lax.axis_size(axis)
    index = lax.axis_index(axis)
    arrived = [
        lax.ppermute(pieces(lax.rem(index + d, size)), axis, shifted(size, d)) for d in (2, 1, 3)
    ]
    total = pieces(index).astype(F32)
    for value in arrived:
        total = total + value.astype(F32)
    return total.astype(out_type)


def halved(pieces, axis):
    size = lax.axis_size(axis)
    index = lax.axis_index(axis)
    own, ahead, across, behind = (pieces(lax.rem(index + d, size)) for d in (0, 1, 2, 3))
    cut = own.shape[0] // 2
    forward, backward = shifted(size, 1), shifted(size, size - 1)
    from_behind = lax.ppermute(jnp.concatenate([across[:cut], ahead[cut:]]), axis, forward)
    from_ahead = lax.ppermute(jnp.concatenate([across[cut:], behind[:cut]]), axis, backward)
    rest = own.shape[0] - cut
    passed_on = lax.ppermute(add(ahead[:cut], from_behind[:cut]), axis, forward)
    passed_back = lax.ppermute(add(behind[cut:], from_ahead[:rest]), axis, backward)
    low = add(own[:cut], from_ahead[rest:], passed_on)
    high = add(own[cut:], from_behind[cut:], passed_back)
    return jnp.concatenate([low, high])


def add(*terms):
    total = terms[0].astype(F32)
    for term in terms[1:]:
        total = total + term.astype(F32)
    return total.astype(BF16)


def take(value, index, dim):
    return lax.dynamic_index_in_dim(value, index, dim, keepdims=False)


def per_device(
    latents, cotangent, timesteps, layer_count, up_weight, down_weight, time_weight, skip_weight
):
    sections = lax.axis_size("pipe")
    stage = lax.axis_index("pipe")
    core = lax.axis_index("core")
    samples, rows, width = latents.shape
    up, down, skip_mat = up_weight[0], down_weight[0].swapaxes(1, 2), skip_weight[0]
    slots, _, hidden_width = up.shape
    scal = jnp.stack([stage, layer_count[0], core, core]).astype(jnp.int32)
    condition = jax.nn.silu(embedding(timesteps, width // 2)).astype(BF16)
    modulation = jnp.einsum("mt,jtc->mjc", condition, time_weight[0], preferred_element_type=F32)
    order_x = block_order(width, "x", "y")
    order_y = block_order(width, "y", "x")

    def columns(order):
        placed = lax.dot_general(order, condition, (((0,), (1,)), ((), ())))
        return placed.astype(F32)

    condition_x, condition_y = columns(order_x), columns(order_y)

    ticks = samples + 2 * (sections - 1)
    empty = jnp.zeros((rows, width), BF16)
    moved = {}
    skips_moved = {}
    saved = None
    for tick in range(ticks):
        incoming = moved.get(tick - 2, empty)
        sent, saved = forward_call(
            tick,
            scal,
            modulation,
            latents,
            incoming,
            up,
            down,
            skip_mat,
            skips_moved.get(tick - 2 * (sections - 1)),
            saved,
        )
        pairs = [(z, z + 1) for z in range(sections - 1) if 0 <= tick - 2 * z < samples]
        if pairs:
            moved[tick] = lax.ppermute(sent, "pipe", pairs)
        if tick < samples:
            skips_moved[tick] = lax.ppermute(sent, "pipe", [(0, sections - 1)])
    states, pres, skips = saved

    moved = {}
    skips_moved = {}
    kept = None
    for tick in range(ticks):
        incoming = moved.get(tick - 2, empty)
        sent, sent_skip, kept = backward_call(
            tick,
            scal,
            modulation,
            cotangent,
            incoming,
            up,
            down,
            skip_mat,
            states,
            pres,
            skips_moved.get(tick - 2 * (sections - 1)),
            kept,
        )
        pairs = [
            (z, z - 1)
            for z in range(1, sections)
            if 0 <= tick - 2 * (sections - 1 - z) < samples
        ]
        if pairs:
            moved[tick] = lax.ppermute(sent, "pipe", pairs)
        if tick < samples:
            skips_moved[tick] = lax.ppermute(sent_skip, "pipe", [(sections - 1, 0)])
    norms, outs, hiddens, dpres, mod_grads, firsts = kept
    total_rows = samples * rows

    mine_up, theirs_up = up_grad_call(
        scal,
        norms.reshape(slots, total_rows, width),
        dpres.reshape(slots, total_rows, hidden_width),
        order_x,
        condition_x,
        mod_grads,
    )
    other_up = lax.ppermute(theirs_up, "core", [(0, 1), (1, 0)])
    mine_down, theirs_down = down_grad_call(
        scal,
        hiddens.reshape(slots, total_rows, hidden_width),
        outs.reshape(slots, total_rows, width),
        skips.reshape(total_rows, width),
        firsts.reshape(total_rows, width),
        order_y,
        condition_y,
        mod_grads,
    )
    other_down = lax.ppermute(theirs_down, "core", [(0, 1), (1, 0)])

    sum_up = halved(lambda i: add(take(mine_up, i, 0), take(other_up, i, 0)), "x")
    sum_down = halved(lambda i: add(take(mine_down, i, 0), take(other_down, i, 0)), "y")
    block, part = width // 8, width // 32
    blocks = 2 * slots
    down_part = sum_down[:blocks].reshape(slots, 2, block, 2, width).transpose(1, 3, 0, 2, 4)
    down_part = down_part.reshape(4, slots * block, width)
    time_part = sum_down[blocks].reshape(4, part, 2, width).transpose(0, 2, 1, 3)
    skip_part = sum_down[blocks + 1, :, :width].reshape(4, part, width)
    down_part = jnp.concatenate(
        [down_part, time_part.reshape(4, 2 * part, width), skip_part], axis=1
    )
    up_part = sum_up.reshape(blocks + 2, 4, part, 2 * width)

    final_up = scattered(lambda i: take(up_part, i, 1), "y", F32)
    final_down = scattered(lambda i: take(down_part, i, 0), "x", F32)
    grad_up = final_up[:blocks].reshape(slots, 2, part, 2 * width).transpose(0, 2, 1, 3)
    grad_up = grad_up.reshape(slots, part, hidden_width)
    grad_down = final_down[: slots * block].reshape(slots, block, width)
    last_time = final_down[slots * block : slots * block + 2 * part].reshape(2, part, width)
    last_time = last_time.transpose(1, 0, 2).reshape(1, part, 2 * width)
    grad_time = jnp.concatenate([final_up[blocks:], last_time])
    grad_skip = final_down[slots * block + 2 * part :]
    return (grad_up[None], grad_down[None], grad_time[None], grad_skip[None])


def solution(mesh):
    split = Mesh(
        mesh.devices.reshape(4, 4, 2, mesh.devices.shape[1]), ("y", "x", "core", "pipe")
    )
    dp = ("y", "x", "core")
    placed = (
        P(dp, None, None),
        P(dp, None, None),
        P(dp),
        P("pipe"),
        P("pipe", None, None, None),
        P("pipe", None, None, None),
        P("pipe", None, None, None),
        P("pipe", None, None),
    )
    return jax.shard_map(
        per_device,
        mesh=split,
        in_specs=placed,
        out_specs=(
            P("pipe", None, dp, None),
            P("pipe", None, dp, None),
            P("pipe", None, dp, None),
            P("pipe", dp, None),
        ),
        check_vma=False,
    )
```

```python
import functools
import math

import jax
import jax.numpy as jnp
import ml_dtypes
import numpy as np
from jax import lax
from jax.experimental import pallas as pl
from jax.experimental.pallas import tpu as pltpu
from jax.sharding import Mesh
from jax.sharding import PartitionSpec as P

EPSILON = 1e-06
BF16 = jnp.bfloat16
F32 = jnp.float32
CHUNK = 256
SECTION_VMEM = 53 * 1024 * 1024
GRAD_VMEM = 56 * 1024 * 1024
ANY = pl.BlockSpec(memory_space=pl.ANY)
VMEM = pl.BlockSpec(memory_space=pltpu.VMEM)
SMEM = pl.BlockSpec(memory_space=pltpu.SMEM)
NT = (((1,), (1,)), ((), ()))
TN = (((0,), (0,)), ((), ()))


def embedding(timesteps, halfway):
    frequency = jnp.exp(-math.log(10000.0) * jnp.arange(halfway, dtype=F32) / halfway)
    angles = timesteps.astype(F32)[..., None] * frequency
    return jnp.concatenate([jnp.sin(angles), jnp.cos(angles)], axis=-1)


def nt_dot(left, right):
    return lax.dot_general(left, right, NT, preferred_element_type=F32)


def sigmoid(value):
    return 0.5 * jnp.tanh(0.5 * value) + 0.5


def backward_layers(count, sample, slots, width, buffers, targets, sems, base, loads):
    modv, upv, downv, statev, prev, acc, nv, ov, hidv, dpv, mgv, fv = buffers
    norms, outs, hiddens, dpres, mod_grads, firsts = targets
    hidden_width = upv.shape[2]

    def saves(j):
        pairs = (
            (nv.at[j], norms.at[j, sample]),
            (ov.at[j], outs.at[j, sample]),
            (hidv.at[j], hiddens.at[j, sample]),
            (dpv.at[j], dpres.at[j, sample]),
        )
        return [
            pltpu.make_async_copy(source, target, sems.at[base + group * slots + j])
            for group, (source, target) in enumerate(pairs)
        ]

    mgv[...] = jnp.zeros_like(mgv)

    @pl.loop(0, count)
    def _(i):
        j = count - 1 - i
        for load in loads(j):
            load.wait()
        grad = acc[...]
        grad_b = grad.astype(BF16)
        ov[j] = grad_b
        for start in range(0, hidden_width, CHUNK):
            cols = slice(start, start + CHUNK)
            grad_hidden = jnp.dot(grad_b, downv[j, :, cols], preferred_element_type=F32)
            pre = prev[j, :, cols].astype(F32)
            gate = sigmoid(pre)
            hidden = pre * gate
            hidv[j, :, cols] = hidden.astype(BF16)
            dpv[j, :, cols] = (grad_hidden * (gate + hidden * (1.0 - gate))).astype(BF16)
        total = nt_dot(dpv[j], upv[j])
        state = statev[j]
        scaling = 1.0 + modv[pl.ds(j, 1), :width]
        offset = modv[pl.ds(j, 1), width:]
        inverse = lax.rsqrt(jnp.mean(state * state, axis=-1, keepdims=True) + EPSILON)
        unit = state * inverse
        nv[j] = (unit * scaling + offset).astype(BF16)
        grad_norm = total.astype(BF16).astype(F32)
        scaled = grad_norm * unit
        mgv[pl.ds(j, 1), :width] = jnp.sum(scaled, axis=0, keepdims=True)
        mgv[pl.ds(j, 1), width:] = jnp.sum(grad_norm, axis=0, keepdims=True)
        inner = jnp.mean(scaled * scaling, axis=-1, keepdims=True)
        acc[...] = grad + inverse * (grad_norm * scaling - unit * inner)
        for save in saves(j):
            save.start()

    first = acc[...].astype(BF16)
    fv[...] = first
    save_mods = pltpu.make_async_copy(mgv, mod_grads.at[sample], sems.at[base + 4 * slots])
    save_first = pltpu.make_async_copy(fv, firsts.at[sample], sems.at[base + 4 * slots + 1])
    save_mods.start()
    save_first.start()

    def finish():
        @pl.loop(0, count)
        def _(j):
            for save in saves(j):
                save.wait()

        save_first.wait()
        save_mods.wait()

    return first, finish


def forward_kernel(
    tick, has_saved, has_skip, has_kept, samples, slots, sections, width, *refs
):
    refs = list(refs)
    scal, mod, latents, incoming, up, down, skip_weight = refs[:7]
    del refs[:7]
    skip_in = refs.pop(0) if has_skip else None
    cotangent = refs.pop(0) if has_skip else None
    if has_saved:
        del refs[:3]
    if has_kept:
        del refs[:6]
    out, states, pres, skips = refs[:4]
    del refs[:4]
    if has_skip:
        out_skip, *targets = refs[:7]
        del refs[:7]
    sems = refs.pop()
    xv, sv, modv, upv, downv, skwv, statev, prev, acc, hidv = refs[:10]
    spare = refs[10:]
    stage, count = scal[0], scal[1]
    sample = tick - 2 * stage
    hidden_width = upv.shape[2]
    half = sections // 2

    @pl.when((sample >= 0) & (sample < samples))
    def _():
        copy_latents = pltpu.make_async_copy(latents.at[sample], xv, sems.at[0])
        copy_incoming = pltpu.make_async_copy(incoming, xv, sems.at[0])
        copy_mod = pltpu.make_async_copy(mod.at[sample], modv, sems.at[1])
        copy_skw = pltpu.make_async_copy(skip_weight, skwv, sems.at[2])

        def copy_up(j):
            return pltpu.make_async_copy(up.at[j], upv.at[j], sems.at[4 + j])

        def copy_down(j):
            return pltpu.make_async_copy(down.at[j], downv.at[j], sems.at[4 + slots + j])

        def save_state(j):
            return pltpu.make_async_copy(
                statev.at[j], states.at[sample, j], sems.at[4 + 2 * slots + j]
            )

        def save_pre(j):
            return pltpu.make_async_copy(prev.at[j], pres.at[sample, j], sems.at[4 + 3 * slots + j])

        save_skip = pltpu.make_async_copy(sv, skips.at[sample], sems.at[3])

        @pl.when(stage == 0)
        def _():
            copy_latents.start()

        @pl.when(stage != 0)
        def _():
            copy_incoming.start()

        copy_mod.start()
        decoder = stage >= half
        if has_skip:
            base = 4 + 4 * slots
            copy_cot = pltpu.make_async_copy(
                cotangent.at[sample], spare[0], sems.at[base + 4 * slots + 2]
            )

            @pl.when(stage == sections - 1)
            def _():
                copy_cot.start()

        @pl.when(decoder)
        def _():
            copy_skw.start()

        @pl.loop(0, count)
        def _(j):
            copy_up(j).start()
            copy_down(j).start()

        copy_incoming.wait()
        acc[...] = xv[...].astype(F32)

        @pl.when(decoder)
        def _():
            if has_skip:
                copy_skip = pltpu.make_async_copy(skip_in, sv, sems.at[3])

                @pl.when(stage == sections - 1)
                def _():
                    copy_skip.start()
                    copy_skip.wait()

                @pl.when(stage != sections - 1)
                def _():
                    sv[...] = xv[...]

            else:
                sv[...] = xv[...]
            save_skip.start()
            copy_skw.wait()
            acc[...] += jnp.dot(sv[...], skwv[...], preferred_element_type=F32)

        copy_mod.wait()

        @pl.loop(0, count)
        def _(j):
            copy_up(j).wait()
            copy_down(j).wait()
            state = acc[...]
            statev[j] = state
            scaling = modv[pl.ds(j, 1), :width]
            offset = modv[pl.ds(j, 1), width:]
            inverse = lax.rsqrt(jnp.mean(state * state, axis=-1, keepdims=True) + EPSILON)
            normed = (state * inverse * (1.0 + scaling) + offset).astype(BF16)
            for start in range(0, hidden_width, CHUNK):
                cols = slice(start, start + CHUNK)
                pre = jnp.dot(normed, upv[j, :, cols], preferred_element_type=F32)
                prev[j, :, cols] = pre.astype(BF16)
                hidv[:, cols] = (pre * sigmoid(pre)).astype(BF16)
            acc[...] = state + nt_dot(hidv[...], downv[j])
            if has_skip:

                @pl.when(stage != sections - 1)
                def _():
                    save_state(j).start()
                    save_pre(j).start()

            else:
                save_state(j).start()
                save_pre(j).start()

        def hand_on():
            xv[...] = acc[...].astype(BF16)
            save_out.start()

            @pl.loop(0, count)
            def _(j):
                save_state(j).wait()
                save_pre(j).wait()

        def turn_back():
            cv, gsv, *layers = spare
            copy_cot.wait()
            acc[...] = cv[...].astype(F32)
            first, finish = backward_layers(
                count,
                sample,
                slots,
                width,
                (modv, upv, downv, statev, prev, acc, *layers),
                targets,
                sems,
                base,
                lambda j: (),
            )
            xv[...] = first
            save_out.start()
            gsv[...] = nt_dot(first, skwv[...]).astype(BF16)
            save_grad = pltpu.make_async_copy(gsv, out_skip, sems.at[base + 4 * slots + 2])
            save_grad.start()
            finish()
            save_grad.wait()

        save_out = pltpu.make_async_copy(xv, out, sems.at[0])
        if has_skip:
            pl.when(stage == sections - 1)(turn_back)
            pl.when(stage != sections - 1)(hand_on)
        else:
            hand_on()

        @pl.when(decoder)
        def _():
            save_skip.wait()

        save_out.wait()


def forward_call(
    tick, scal, mod, latents, incoming, up, down, skip_weight, skip_in, cotangent, saved, kept
):
    samples, rows, width = latents.shape
    slots, _, hidden_width = up.shape
    shapes = (
        jax.ShapeDtypeStruct((rows, width), BF16),
        jax.ShapeDtypeStruct((samples, slots, rows, width), F32),
        jax.ShapeDtypeStruct((samples, slots, rows, hidden_width), BF16),
        jax.ShapeDtypeStruct((samples, rows, width), BF16),
    )
    scratch = []
    if skip_in is not None:
        shapes += (jax.ShapeDtypeStruct((rows, width), BF16),)
        shapes += kept_shapes(samples, slots, rows, width, hidden_width)
        scratch = [pltpu.VMEM((rows, width), BF16)] * 2
        scratch += layer_scratch(slots, rows, width, hidden_width)
    operands = [scal, mod, latents, incoming, up, down, skip_weight]
    if skip_in is not None:
        operands += [skip_in, cotangent]
    aliases = {}
    if saved is not None:
        aliases = {len(operands) + i: 1 + i for i in range(3)}
        operands += list(saved)
    if kept is not None:
        aliases |= {len(operands) + i: 5 + i for i in range(6)}
        operands += list(kept)
    out = pl.pallas_call(
        functools.partial(
            forward_kernel,
            tick,
            saved is not None,
            skip_in is not None,
            kept is not None,
            samples,
            slots,
            4,
            width,
        ),
        out_shape=shapes,
        in_specs=[SMEM] + [ANY] * (len(operands) - 1),
        out_specs=(ANY,) * len(shapes),
        input_output_aliases=aliases,
        scratch_shapes=[
            pltpu.VMEM((rows, width), BF16),
            pltpu.VMEM((rows, width), BF16),
            pltpu.VMEM((slots, 2 * width), F32),
            pltpu.VMEM((slots, width, hidden_width), BF16),
            pltpu.VMEM((slots, width, hidden_width), BF16),
            pltpu.VMEM((width, width), BF16),
            pltpu.VMEM((slots, rows, width), F32),
            pltpu.VMEM((slots, rows, hidden_width), BF16),
            pltpu.VMEM((rows, width), F32),
            pltpu.VMEM((rows, hidden_width), BF16),
            *scratch,
            pltpu.SemaphoreType.DMA((7 + 8 * slots,)),
        ],
        compiler_params=pltpu.CompilerParams(vmem_limit_bytes=SECTION_VMEM),
        cost_estimate=pl.CostEstimate(
            flops=slots * rows * width * hidden_width * 4,
            bytes_accessed=8_000_000,
            transcendentals=0,
        ),
        name=f"section_forward_{tick}",
    )(*operands)
    return out[0], out[1:4], out[4:5], out[5:]


def kept_shapes(samples, slots, rows, width, hidden_width):
    narrow = jax.ShapeDtypeStruct((slots, samples, rows, width), BF16)
    wide = jax.ShapeDtypeStruct((slots, samples, rows, hidden_width), BF16)
    return (
        narrow,
        narrow,
        wide,
        wide,
        jax.ShapeDtypeStruct((samples, slots, 2 * width), F32),
        jax.ShapeDtypeStruct((samples, rows, width), BF16),
    )


def layer_scratch(slots, rows, width, hidden_width):
    return [
        pltpu.VMEM((slots, rows, width), BF16),
        pltpu.VMEM((slots, rows, width), BF16),
        pltpu.VMEM((slots, rows, hidden_width), BF16),
        pltpu.VMEM((slots, rows, hidden_width), BF16),
        pltpu.VMEM((slots, 2 * width), F32),
        pltpu.VMEM((rows, width), BF16),
    ]


def backward_kernel(tick, has_top, has_skip, samples, slots, sections, width, *refs):
    refs = list(refs)
    scal, mod, incoming, up, down, skip_weight, states, pres = refs[:8]
    del refs[:8]
    top = refs.pop(0) if has_top else None
    skip_grad = refs.pop(0) if has_skip else None
    del refs[:6]
    out, *targets = refs[:7]
    gv, hv, modv, upv, downv, skwv, statev, prev, acc, *layers, sems = refs[7:]
    stage, count = scal[0], scal[1]
    sample = tick - 2 * (sections - 1 - stage)
    half = sections // 2

    @pl.when((sample >= 0) & (sample < samples) & (stage != sections - 1))
    def _():
        copy_incoming = pltpu.make_async_copy(incoming, gv, sems.at[0])
        copy_mod = pltpu.make_async_copy(mod.at[sample], modv, sems.at[1])
        copy_skw = pltpu.make_async_copy(skip_weight, skwv, sems.at[2])

        def copy(group, j, source, target):
            return pltpu.make_async_copy(source, target, sems.at[4 + group * slots + j])

        def loads(j):
            return (
                copy(0, j, down.at[j], downv.at[j]),
                copy(1, j, pres.at[sample, j], prev.at[j]),
                copy(2, j, up.at[j], upv.at[j]),
                copy(3, j, states.at[sample, j], statev.at[j]),
            )

        if has_top:
            copy_top = pltpu.make_async_copy(top, gv, sems.at[0])

            @pl.when(stage == sections - 2)
            def _():
                copy_top.start()

            @pl.when(stage != sections - 2)
            def _():
                copy_incoming.start()

        else:
            copy_incoming.start()
        if has_skip:
            copy_skip = pltpu.make_async_copy(skip_grad, hv, sems.at[3])

            @pl.when(stage == 0)
            def _():
                copy_skip.start()

        copy_mod.start()
        decoder = stage >= half

        @pl.loop(0, count)
        def _(i):
            for load in loads(count - 1 - i):
                load.start()

        @pl.when(decoder)
        def _():
            copy_skw.start()

        copy_incoming.wait()
        if has_skip:

            @pl.when(stage == 0)
            def _():
                copy_skip.wait()
                acc[...] = (gv[...] + hv[...]).astype(F32)

            @pl.when(stage != 0)
            def _():
                acc[...] = gv[...].astype(F32)

        else:
            acc[...] = gv[...].astype(F32)
        copy_mod.wait()
        first, finish = backward_layers(
            count,
            sample,
            slots,
            width,
            (modv, upv, downv, statev, prev, acc, *layers),
            targets,
            sems,
            4 + 4 * slots,
            loads,
        )
        gv[...] = first

        @pl.when(decoder)
        def _():
            copy_skw.wait()
            gv[...] = first + nt_dot(first, skwv[...]).astype(BF16)

        save_down = pltpu.make_async_copy(gv, out, sems.at[0])
        save_down.start()
        finish()
        save_down.wait()


def backward_call(tick, scal, mod, incoming, up, down, skip_weight, saved, top, skip_grad, kept):
    states, pres, _ = saved
    samples, slots, rows, width = states.shape
    hidden_width = up.shape[2]
    narrow = (rows, width)
    wide = (rows, hidden_width)
    shapes = (jax.ShapeDtypeStruct(narrow, BF16),)
    shapes += kept_shapes(samples, slots, rows, width, hidden_width)
    operands = [scal, mod, incoming, up, down, skip_weight, states, pres]
    if top is not None:
        operands.append(top)
    if skip_grad is not None:
        operands.append(skip_grad)
    aliases = {len(operands) + i: 1 + i for i in range(6)}
    operands += list(kept)
    out = pl.pallas_call(
        functools.partial(
            backward_kernel,
            tick,
            top is not None,
            skip_grad is not None,
            samples,
            slots,
            4,
            width,
        ),
        out_shape=shapes,
        in_specs=[SMEM] + [ANY] * (len(operands) - 1),
        out_specs=(ANY,) * len(shapes),
        input_output_aliases=aliases,
        scratch_shapes=[
            pltpu.VMEM(narrow, BF16),
            pltpu.VMEM(narrow, BF16),
            pltpu.VMEM((slots, 2 * width), F32),
            pltpu.VMEM((slots, width, hidden_width), BF16),
            pltpu.VMEM((slots, width, hidden_width), BF16),
            pltpu.VMEM((width, width), BF16),
            pltpu.VMEM((slots, *narrow), F32),
            pltpu.VMEM((slots, *wide), BF16),
            pltpu.VMEM(narrow, F32),
            *layer_scratch(slots, rows, width, hidden_width),
            pltpu.SemaphoreType.DMA((6 + 8 * slots,)),
        ],
        compiler_params=pltpu.CompilerParams(vmem_limit_bytes=SECTION_VMEM),
        cost_estimate=pl.CostEstimate(
            flops=slots * rows * width * hidden_width * 4,
            bytes_accessed=14_000_000,
            transcendentals=0,
        ),
        name=f"section_backward_{tick}",
    )(*operands)
    return out[0], out[1:]


def time_product(condition, order, mod_grads, slot):
    placed = jnp.dot(condition[...], order[...], preferred_element_type=F32)
    samples, _, lanes = mod_grads.shape
    grads = [mod_grads[sample, slot : slot + 1, :] for sample in range(samples)]
    grads.append(jnp.zeros((condition.shape[0] - samples, lanes), F32))
    return lax.dot_general(
        placed, jnp.concatenate(grads, axis=0), TN, preferred_element_type=F32
    )


def up_grad_kernel(
    scal, norms, dpres, order, condition, mod_grads, mine, theirs, nv, dv, product, packed, sems
):
    count, core = scal[1], scal[2]
    slots = nv.shape[0]
    block, lanes = mine.shape[2:]

    def loads(j):
        return (
            pltpu.make_async_copy(norms.at[j], nv.at[j], sems.at[0, j]),
            pltpu.make_async_copy(dpres.at[j], dv.at[j], sems.at[1, j]),
        )

    def saves(j):
        place = pl.ds(2 * j, 2)
        return (
            pltpu.make_async_copy(packed.at[1, j], theirs.at[:, place], sems.at[2, j]),
            pltpu.make_async_copy(packed.at[0, j], mine.at[:, place], sems.at[3, j]),
        )

    def pack(j):
        for target, side in ((1, 1 - core), (0, core)):
            for i in range(4):
                for half in range(2):
                    low = pl.multiple_of((side * 4 + i) * block, 8)
                    cols = slice(half * lanes, (half + 1) * lanes)
                    packed[target, j, i, half] = product[pl.ds(low, block), cols].astype(BF16)

    @pl.loop(0, count)
    def _(j):
        for load in loads(j):
            load.start()

    for half in range(2):
        product[:, half * lanes : (half + 1) * lanes] = time_product(
            condition, order, mod_grads, half
        )

    pack(slots)
    for save in saves(slots):
        save.start()

    @pl.loop(0, slots)
    def _(j):
        @pl.when(j < count)
        def _():
            for load in loads(j):
                load.wait()
            placed = jnp.dot(nv[j], order[...], preferred_element_type=F32).astype(BF16)
            product[...] = jnp.dot(placed.T, dv[j], preferred_element_type=F32)
            pack(j)

        @pl.when(j >= count)
        def _():
            for target in range(2):
                packed[target, j] = jnp.zeros(packed.shape[2:], BF16)

        for save in saves(j):
            save.start()

    @pl.loop(0, slots + 1)
    def _(j):
        for save in saves(j):
            save.wait()


def up_grad_call(scal, norms, dpres, order, condition, mod_grads):
    slots, rows, width = norms.shape
    hidden_width = dpres.shape[2]
    block = width // 8
    shape = jax.ShapeDtypeStruct((4, 2 * slots + 2, block, hidden_width // 2), BF16)
    return pl.pallas_call(
        up_grad_kernel,
        out_shape=(shape, shape),
        in_specs=[SMEM, ANY, ANY, VMEM, VMEM, VMEM],
        out_specs=(ANY, ANY),
        scratch_shapes=[
            pltpu.VMEM((slots, rows, width), BF16),
            pltpu.VMEM((slots, rows, hidden_width), BF16),
            pltpu.VMEM((width, hidden_width), F32),
            pltpu.VMEM((2, slots + 1, 4, 2, block, hidden_width // 2), BF16),
            pltpu.SemaphoreType.DMA((4, slots + 1)),
        ],
        compiler_params=pltpu.CompilerParams(vmem_limit_bytes=GRAD_VMEM),
        cost_estimate=pl.CostEstimate(
            flops=2 * slots * rows * width * hidden_width,
            bytes_accessed=12_000_000,
            transcendentals=0,
        ),
        name="up_grad",
    )(scal, norms, dpres, order, condition, mod_grads)


def down_grad_kernel(
    scal,
    hiddens,
    outs,
    skips,
    firsts,
    order,
    condition,
    mod_grads,
    mine,
    theirs,
    hv,
    gv,
    sv,
    fv,
    product,
    prod_time,
    prod_skip,
    packed,
    sems,
):
    stage, count, core = scal[0], scal[1], scal[2]
    slots = hv.shape[0]
    block, lanes = mine.shape[2:]
    width = lanes // 2
    load_skip = pltpu.make_async_copy(skips, sv, sems.at[0, slots])
    load_first = pltpu.make_async_copy(firsts, fv, sems.at[1, slots])

    def loads(j):
        return (
            pltpu.make_async_copy(hiddens.at[j], hv.at[j], sems.at[0, j]),
            pltpu.make_async_copy(outs.at[j], gv.at[j], sems.at[1, j]),
        )

    def saves(j):
        place = pl.ds(2 * j, 2)
        return (
            pltpu.make_async_copy(packed.at[1, j], theirs.at[:, place], sems.at[2, j]),
            pltpu.make_async_copy(packed.at[0, j], mine.at[:, place], sems.at[3, j]),
        )

    @pl.when(stage >= 2)
    def _():
        load_skip.start()
        load_first.start()

    @pl.loop(0, count)
    def _(j):
        for load in loads(j):
            load.start()

    prod_time[...] = time_product(condition, order, mod_grads, slots - 1)
    prod_skip[...] = jnp.zeros_like(prod_skip)

    @pl.when(stage >= 2)
    def _():
        load_skip.wait()
        load_first.wait()
        placed = jnp.dot(sv[...], order[...], preferred_element_type=F32).astype(BF16)
        prod_skip[:, :width] = lax.dot_general(placed, fv[...], TN, preferred_element_type=F32)

    for target, side in ((1, 1 - core), (0, core)):
        for y in range(4):
            low = pl.multiple_of((side * 4 + y) * block, 8)
            packed[target, slots, y, 0] = prod_time[pl.ds(low, block), :].astype(BF16)
            packed[target, slots, y, 1] = prod_skip[pl.ds(low, block), :].astype(BF16)
    for save in saves(slots):
        save.start()

    @pl.loop(0, slots)
    def _(j):
        @pl.when(j < count)
        def _():
            for load in loads(j):
                load.wait()
            for start in range(0, hv.shape[2], CHUNK):
                cols = slice(start, start + CHUNK)
                product[cols, :] = lax.dot_general(
                    hv[j, :, cols], gv[j], TN, preferred_element_type=F32
                )
            for target, side in ((1, 1 - core), (0, core)):
                for y in range(4):
                    for pair in range(2):
                        low = pl.multiple_of((8 * y + 4 * pair + side) * block, 8)
                        high = pl.multiple_of((8 * y + 4 * pair + 2 + side) * block, 8)
                        packed[target, j, y, pair] = jnp.concatenate(
                            [product[pl.ds(low, block), :], product[pl.ds(high, block), :]],
                            axis=1,
                        ).astype(BF16)

        @pl.when(j >= count)
        def _():
            for target in range(2):
                packed[target, j] = jnp.zeros(packed.shape[2:], BF16)

        for save in saves(j):
            save.start()

    @pl.loop(0, slots + 1)
    def _(j):
        for save in saves(j):
            save.wait()


def down_grad_call(scal, hiddens, outs, skips, firsts, order, condition, mod_grads):
    slots, rows, hidden_width = hiddens.shape
    width = outs.shape[2]
    block = width // 8
    shape = jax.ShapeDtypeStruct((4, 2 * slots + 2, block, 2 * width), BF16)
    return pl.pallas_call(
        down_grad_kernel,
        out_shape=(shape, shape),
        in_specs=[SMEM, ANY, ANY, ANY, ANY, VMEM, VMEM, VMEM],
        out_specs=(ANY, ANY),
        scratch_shapes=[
            pltpu.VMEM((slots, rows, hidden_width), BF16),
            pltpu.VMEM((slots, rows, width), BF16),
            pltpu.VMEM((rows, width), BF16),
            pltpu.VMEM((rows, width), BF16),
            pltpu.VMEM((hidden_width, width), F32),
            pltpu.VMEM((width, 2 * width), F32),
            pltpu.VMEM((width, 2 * width), F32),
            pltpu.VMEM((2, slots + 1, 4, 2, block, 2 * width), BF16),
            pltpu.SemaphoreType.DMA((4, slots + 1)),
        ],
        compiler_params=pltpu.CompilerParams(vmem_limit_bytes=GRAD_VMEM),
        cost_estimate=pl.CostEstimate(
            flops=2 * slots * rows * width * hidden_width,
            bytes_accessed=12_000_000,
            transcendentals=0,
        ),
        name="down_grad",
    )(scal, hiddens, outs, skips, firsts, order, condition, mod_grads)


def block_order(width, first, second):
    block = width // 32
    matrix = np.zeros((width, width), ml_dtypes.bfloat16)
    for y in range(4):
        for x in range(4):
            for core in range(2):
                where = {"x": x, "y": y}
                place = (core * 4 + where[first]) * 4 + where[second]
                source = 8 * y + 2 * x + core
                for r in range(block):
                    matrix[source * block + r, place * block + r] = 1
    return jnp.asarray(matrix)


def shifted(size, distance):
    return [(i, (i + distance) % size) for i in range(size)]


def paired(pieces, axis):
    index = lax.axis_index(axis)
    other = 3 - index
    sent = jnp.stack([pieces(index ^ 1), pieces(other ^ 1)])
    arrived = lax.ppermute(sent, axis, [(i, i ^ 1) for i in range(4)])
    passed = add(pieces(other), arrived[1])
    last = lax.ppermute(passed, axis, [(i, 3 - i) for i in range(4)])
    return pieces(index).astype(F32) + arrived[0].astype(F32) + last.astype(F32)


def halved(pieces, axis):
    size = lax.axis_size(axis)
    index = lax.axis_index(axis)
    own, ahead, across, behind = (pieces(lax.rem(index + d, size)) for d in (0, 1, 2, 3))
    cut = own.shape[0] // 2
    forward, backward = shifted(size, 1), shifted(size, size - 1)
    from_behind = lax.ppermute(jnp.concatenate([across[:cut], ahead[cut:]]), axis, forward)
    from_ahead = lax.ppermute(jnp.concatenate([across[cut:], behind[:cut]]), axis, backward)
    rest = own.shape[0] - cut
    passed_on = lax.ppermute(add(ahead[:cut], from_behind[:cut]), axis, forward)
    passed_back = lax.ppermute(add(behind[cut:], from_ahead[:rest]), axis, backward)
    low = add(own[:cut], from_ahead[rest:], passed_on)
    high = add(own[cut:], from_behind[cut:], passed_back)
    return jnp.concatenate([low, high])


def add(*terms):
    total = terms[0].astype(F32)
    for term in terms[1:]:
        total = total + term.astype(F32)
    return total.astype(BF16)


def take(value, index, dim):
    return lax.dynamic_index_in_dim(value, index, dim, keepdims=False)


def per_device(
    latents, cotangent, timesteps, layer_count, up_weight, down_weight, time_weight, skip_weight
):
    sections = lax.axis_size("pipe")
    stage = lax.axis_index("pipe")
    core = lax.axis_index("core")
    samples, rows, width = latents.shape
    up, down, skip_mat = up_weight[0], down_weight[0].swapaxes(1, 2), skip_weight[0]
    slots, _, hidden_width = up.shape
    scal = jnp.stack([stage, layer_count[0], core, core]).astype(jnp.int32)
    condition = jax.nn.silu(embedding(timesteps, width // 2)).astype(BF16)
    modulation = jnp.einsum("mt,jtc->mjc", condition, time_weight[0], preferred_element_type=F32)
    order_x = block_order(width, "x", "y")
    order_y = block_order(width, "y", "x")

    padded = jnp.concatenate([condition, jnp.zeros((16 - samples, width), BF16)])

    lead = 2 * (sections - 1)
    ticks = samples + lead
    empty = jnp.zeros((rows, width), BF16)
    moved, skips_moved, tops, skip_grads = {}, {}, {}, {}
    saved, kept = None, None
    for tick in range(ticks):
        sent, saved, sent_skip, made = forward_call(
            tick,
            scal,
            modulation,
            latents,
            moved.get(tick - 2, empty),
            up,
            down,
            skip_mat,
            skips_moved.get(tick - lead),
            cotangent,
            saved,
            kept,
        )
        pairs = [(z, z + 1) for z in range(sections - 1) if 0 <= tick - 2 * z < samples]
        if pairs:
            moved[tick] = lax.ppermute(sent, "pipe", pairs)
        if tick < samples:
            skips_moved[tick] = lax.ppermute(sent, "pipe", [(0, sections - 1)])
        if tick >= lead:
            kept = made
            tops[tick - lead] = lax.ppermute(sent, "pipe", [(sections - 1, sections - 2)])
            skip_grads[tick - lead] = lax.ppermute(sent_skip[0], "pipe", [(sections - 1, 0)])
    skips = saved[2]

    moved = {}
    for tick in range(2, ticks):
        incoming, top = moved.get(tick - 2), tops.get(tick - 2)
        if incoming is None:
            incoming, top = top, None
        sent, kept = backward_call(
            tick,
            scal,
            modulation,
            incoming,
            up,
            down,
            skip_mat,
            saved,
            top,
            skip_grads.get(tick - lead),
            kept,
        )
        pairs = [
            (z, z - 1)
            for z in range(1, sections - 1)
            if 0 <= tick - 2 * (sections - 1 - z) < samples
        ]
        if pairs:
            moved[tick] = lax.ppermute(sent, "pipe", pairs)
    norms, outs, hiddens, dpres, mod_grads, firsts = kept
    total_rows = samples * rows

    mine_up, theirs_up = up_grad_call(
        scal,
        norms.reshape(slots, total_rows, width),
        dpres.reshape(slots, total_rows, hidden_width),
        order_x,
        padded,
        mod_grads,
    )
    other_up = lax.ppermute(theirs_up, "core", [(0, 1), (1, 0)])
    mine_down, theirs_down = down_grad_call(
        scal,
        hiddens.reshape(slots, total_rows, hidden_width),
        outs.reshape(slots, total_rows, width),
        skips.reshape(total_rows, width),
        firsts.reshape(total_rows, width),
        order_y,
        padded,
        mod_grads,
    )
    other_down = lax.ppermute(theirs_down, "core", [(0, 1), (1, 0)])

    sum_up = halved(lambda i: add(take(mine_up, i, 0), take(other_up, i, 0)), "x")
    sum_down = halved(lambda i: add(take(mine_down, i, 0), take(other_down, i, 0)), "y")
    block, part = width // 8, width // 32
    blocks = 2 * slots
    down_part = sum_down[:blocks].reshape(slots, 2, block, 2, width).transpose(1, 3, 0, 2, 4)
    down_part = down_part.reshape(4, slots * block, width)
    time_part = sum_down[blocks].reshape(4, part, 2, width).transpose(0, 2, 1, 3)
    skip_part = sum_down[blocks + 1, :, :width].reshape(4, part, width)
    down_part = jnp.concatenate(
        [down_part, time_part.reshape(4, 2 * part, width), skip_part], axis=1
    )
    up_part = sum_up.reshape(blocks + 2, 4, part, 2 * width)

    final_up = paired(lambda i: take(up_part, i, 1), "y")
    final_down = paired(lambda i: take(down_part, i, 0), "x")
    grad_up = final_up[:blocks].reshape(slots, 2, part, 2 * width).transpose(0, 2, 1, 3)
    grad_up = grad_up.reshape(slots, part, hidden_width)
    grad_down = final_down[: slots * block].reshape(slots, block, width)
    last_time = final_down[slots * block : slots * block + 2 * part].reshape(2, part, width)
    last_time = last_time.transpose(1, 0, 2).reshape(1, part, 2 * width)
    grad_time = jnp.concatenate([final_up[blocks:], last_time])
    grad_skip = final_down[slots * block + 2 * part :]
    return (grad_up[None], grad_down[None], grad_time[None], grad_skip[None])


def solution(mesh):
    split = Mesh(
        mesh.devices.reshape(4, 4, 2, mesh.devices.shape[1]), ("y", "x", "core", "pipe")
    )
    dp = ("y", "x", "core")
    placed = (
        P(dp, None, None),
        P(dp, None, None),
        P(dp),
        P("pipe"),
        P("pipe", None, None, None),
        P("pipe", None, None, None),
        P("pipe", None, None, None),
        P("pipe", None, None),
    )
    return jax.shard_map(
        per_device,
        mesh=split,
        in_specs=placed,
        out_specs=(
            P("pipe", None, dp, None),
            P("pipe", None, dp, None),
            P("pipe", None, dp, None),
            P("pipe", dp, None),
        ),
        check_vma=False,
    )
```

```python
import functools
import math

import jax
import jax.numpy as jnp
import ml_dtypes
import numpy as np
from jax import lax
from jax.experimental import pallas as pl
from jax.experimental.pallas import tpu as pltpu
from jax.sharding import Mesh
from jax.sharding import PartitionSpec as P

EPSILON = 1e-06
BF16 = jnp.bfloat16
F32 = jnp.float32
CHUNK = 256
SECTION_VMEM = 53 * 1024 * 1024
GRAD_VMEM = 56 * 1024 * 1024
ANY = pl.BlockSpec(memory_space=pl.ANY)
VMEM = pl.BlockSpec(memory_space=pltpu.VMEM)
SMEM = pl.BlockSpec(memory_space=pltpu.SMEM)
NT = (((1,), (1,)), ((), ()))
TN = (((0,), (0,)), ((), ()))


def embedding(timesteps, halfway):
    frequency = jnp.exp(-math.log(10000.0) * jnp.arange(halfway, dtype=F32) / halfway)
    angles = timesteps.astype(F32)[..., None] * frequency
    return jnp.concatenate([jnp.sin(angles), jnp.cos(angles)], axis=-1)


def nt_dot(left, right):
    return lax.dot_general(left, right, NT, preferred_element_type=F32)


def sigmoid(value):
    return 0.5 * jnp.tanh(0.5 * value) + 0.5


def backward_layers(count, sample, slots, width, buffers, targets, sems, base, loads):
    modv, upv, downv, statev, prev, acc, nv, ov, hidv, dpv, mgv, fv = buffers
    norms, outs, hiddens, dpres, mod_grads, firsts = targets
    hidden_width = upv.shape[2]

    def saves(j):
        pairs = (
            (nv.at[j], norms.at[j, sample]),
            (ov.at[j], outs.at[j, sample]),
            (hidv.at[j], hiddens.at[j, sample]),
            (dpv.at[j], dpres.at[j, sample]),
        )
        return [
            pltpu.make_async_copy(source, target, sems.at[base + group * slots + j])
            for group, (source, target) in enumerate(pairs)
        ]

    mgv[...] = jnp.zeros_like(mgv)

    @pl.loop(0, count)
    def _(i):
        j = count - 1 - i
        for load in loads(j):
            load.wait()
        grad = acc[...]
        grad_b = grad.astype(BF16)
        ov[j] = grad_b
        for start in range(0, hidden_width, CHUNK):
            cols = slice(start, start + CHUNK)
            grad_hidden = jnp.dot(grad_b, downv[j, :, cols], preferred_element_type=F32)
            pre = prev[j, :, cols].astype(F32)
            gate = sigmoid(pre)
            hidden = pre * gate
            hidv[j, :, cols] = hidden.astype(BF16)
            dpv[j, :, cols] = (grad_hidden * (gate + hidden * (1.0 - gate))).astype(BF16)
        total = nt_dot(dpv[j], upv[j])
        state = statev[j]
        scaling = 1.0 + modv[pl.ds(j, 1), :width]
        offset = modv[pl.ds(j, 1), width:]
        inverse = lax.rsqrt(jnp.mean(state * state, axis=-1, keepdims=True) + EPSILON)
        unit = state * inverse
        nv[j] = (unit * scaling + offset).astype(BF16)
        grad_norm = total.astype(BF16).astype(F32)
        scaled = grad_norm * unit
        mgv[pl.ds(j, 1), :width] = jnp.sum(scaled, axis=0, keepdims=True)
        mgv[pl.ds(j, 1), width:] = jnp.sum(grad_norm, axis=0, keepdims=True)
        inner = jnp.mean(scaled * scaling, axis=-1, keepdims=True)
        acc[...] = grad + inverse * (grad_norm * scaling - unit * inner)
        for save in saves(j):
            save.start()

    first = acc[...].astype(BF16)
    fv[...] = first
    save_mods = pltpu.make_async_copy(mgv, mod_grads.at[sample], sems.at[base + 4 * slots])
    save_first = pltpu.make_async_copy(fv, firsts.at[sample], sems.at[base + 4 * slots + 1])
    save_mods.start()
    save_first.start()

    def finish():
        @pl.loop(0, count)
        def _(j):
            for save in saves(j):
                save.wait()

        save_first.wait()
        save_mods.wait()

    return first, finish


def forward_kernel(
    tick, has_saved, has_skip, has_kept, samples, slots, sections, width, *refs
):
    refs = list(refs)
    scal, mod, latents, incoming, up, down, skip_weight = refs[:7]
    del refs[:7]
    skip_in = refs.pop(0) if has_skip else None
    cotangent = refs.pop(0) if has_skip else None
    if has_saved:
        del refs[:3]
    if has_kept:
        del refs[:6]
    out, states, pres, skips = refs[:4]
    del refs[:4]
    if has_skip:
        out_skip, *targets = refs[:7]
        del refs[:7]
    sems = refs.pop()
    xv, sv, modv, upv, downv, skwv, statev, prev, acc, hidv = refs[:10]
    spare = refs[10:]
    stage, count = scal[0], scal[1]
    sample = tick - 2 * stage
    hidden_width = upv.shape[2]
    half = sections // 2

    is_last = stage == sections - 1
    mine = is_last if has_skip else jnp.logical_not(is_last)

    @pl.when((sample >= 0) & (sample < samples) & mine)
    def _():
        copy_latents = pltpu.make_async_copy(latents.at[sample], xv, sems.at[0])
        copy_incoming = pltpu.make_async_copy(incoming, xv, sems.at[0])
        copy_mod = pltpu.make_async_copy(mod.at[sample], modv, sems.at[1])
        copy_skw = pltpu.make_async_copy(skip_weight, skwv, sems.at[2])

        def copy_up(j):
            return pltpu.make_async_copy(up.at[j], upv.at[j], sems.at[4 + j])

        def copy_down(j):
            return pltpu.make_async_copy(down.at[j], downv.at[j], sems.at[4 + slots + j])

        def save_state(j):
            return pltpu.make_async_copy(
                statev.at[j], states.at[sample, j], sems.at[4 + 2 * slots + j]
            )

        def save_pre(j):
            return pltpu.make_async_copy(prev.at[j], pres.at[sample, j], sems.at[4 + 3 * slots + j])

        save_skip = pltpu.make_async_copy(sv, skips.at[sample], sems.at[3])

        @pl.when(stage == 0)
        def _():
            copy_latents.start()

        @pl.when(stage != 0)
        def _():
            copy_incoming.start()

        copy_mod.start()
        decoder = stage >= half
        if has_skip:
            base = 4 + 4 * slots
            copy_cot = pltpu.make_async_copy(
                cotangent.at[sample], spare[0], sems.at[base + 4 * slots + 2]
            )

            copy_cot.start()
            copy_skip = pltpu.make_async_copy(skip_in, sv, sems.at[3])
            copy_skip.start()

        @pl.when(decoder)
        def _():
            copy_skw.start()

        @pl.loop(0, count)
        def _(j):
            copy_up(j).start()
            copy_down(j).start()

        copy_incoming.wait()
        acc[...] = xv[...].astype(F32)

        @pl.when(decoder)
        def _():
            if has_skip:
                copy_skip.wait()
            else:
                sv[...] = xv[...]
            save_skip.start()
            copy_skw.wait()
            acc[...] += jnp.dot(sv[...], skwv[...], preferred_element_type=F32)

        copy_mod.wait()

        @pl.loop(0, count)
        def _(j):
            copy_up(j).wait()
            copy_down(j).wait()
            state = acc[...]
            statev[j] = state
            scaling = modv[pl.ds(j, 1), :width]
            offset = modv[pl.ds(j, 1), width:]
            inverse = lax.rsqrt(jnp.mean(state * state, axis=-1, keepdims=True) + EPSILON)
            normed = (state * inverse * (1.0 + scaling) + offset).astype(BF16)
            for start in range(0, hidden_width, CHUNK):
                cols = slice(start, start + CHUNK)
                pre = jnp.dot(normed, upv[j, :, cols], preferred_element_type=F32)
                prev[j, :, cols] = pre.astype(BF16)
                hidv[:, cols] = (pre * sigmoid(pre)).astype(BF16)
            acc[...] = state + nt_dot(hidv[...], downv[j])
            if not has_skip:
                save_state(j).start()
                save_pre(j).start()

        def hand_on():
            xv[...] = acc[...].astype(BF16)
            save_out.start()

            @pl.loop(0, count)
            def _(j):
                save_state(j).wait()
                save_pre(j).wait()

        def turn_back():
            cv, gsv, *layers = spare
            copy_cot.wait()
            acc[...] = cv[...].astype(F32)
            first, finish = backward_layers(
                count,
                sample,
                slots,
                width,
                (modv, upv, downv, statev, prev, acc, *layers),
                targets,
                sems,
                base,
                lambda j: (),
            )
            xv[...] = first
            save_out.start()
            gsv[...] = nt_dot(first, skwv[...]).astype(BF16)
            save_grad = pltpu.make_async_copy(gsv, out_skip, sems.at[base + 4 * slots + 2])
            save_grad.start()
            finish()
            save_grad.wait()

        save_out = pltpu.make_async_copy(xv, out, sems.at[0])
        if has_skip:
            turn_back()
        else:
            hand_on()

        @pl.when(decoder)
        def _():
            save_skip.wait()

        save_out.wait()


def forward_call(
    tick, scal, mod, latents, incoming, up, down, skip_weight, skip_in, cotangent, saved, kept
):
    samples, rows, width = latents.shape
    slots, _, hidden_width = up.shape
    shapes = (
        jax.ShapeDtypeStruct((rows, width), BF16),
        jax.ShapeDtypeStruct((samples, slots, rows, width), F32),
        jax.ShapeDtypeStruct((samples, slots, rows, hidden_width), BF16),
        jax.ShapeDtypeStruct((samples, rows, width), BF16),
    )
    scratch = []
    if skip_in is not None:
        shapes += (jax.ShapeDtypeStruct((rows, width), BF16),)
        shapes += kept_shapes(samples, slots, rows, width, hidden_width)
        scratch = [pltpu.VMEM((rows, width), BF16)] * 2
        scratch += layer_scratch(slots, rows, width, hidden_width)
    operands = [scal, mod, latents, incoming, up, down, skip_weight]
    if skip_in is not None:
        operands += [skip_in, cotangent]
    aliases = {}
    if saved is not None:
        aliases = {len(operands) + i: 1 + i for i in range(3)}
        operands += list(saved)
    if kept is not None:
        aliases |= {len(operands) + i: 5 + i for i in range(6)}
        operands += list(kept)
    out = pl.pallas_call(
        functools.partial(
            forward_kernel,
            tick,
            saved is not None,
            skip_in is not None,
            kept is not None,
            samples,
            slots,
            4,
            width,
        ),
        out_shape=shapes,
        in_specs=[SMEM] + [ANY] * (len(operands) - 1),
        out_specs=(ANY,) * len(shapes),
        input_output_aliases=aliases,
        scratch_shapes=[
            pltpu.VMEM((rows, width), BF16),
            pltpu.VMEM((rows, width), BF16),
            pltpu.VMEM((slots, 2 * width), F32),
            pltpu.VMEM((slots, width, hidden_width), BF16),
            pltpu.VMEM((slots, width, hidden_width), BF16),
            pltpu.VMEM((width, width), BF16),
            pltpu.VMEM((slots, rows, width), F32),
            pltpu.VMEM((slots, rows, hidden_width), BF16),
            pltpu.VMEM((rows, width), F32),
            pltpu.VMEM((rows, hidden_width), BF16),
            *scratch,
            pltpu.SemaphoreType.DMA((7 + 8 * slots,)),
        ],
        compiler_params=pltpu.CompilerParams(vmem_limit_bytes=SECTION_VMEM),
        cost_estimate=pl.CostEstimate(
            flops=slots * rows * width * hidden_width * 4,
            bytes_accessed=8_000_000,
            transcendentals=0,
        ),
        name=f"section_forward_{tick}" if skip_in is None else f"section_last_{tick}",
    )(*operands)
    return out[0], out[1:4], out[4:5], out[5:]


def kept_shapes(samples, slots, rows, width, hidden_width):
    narrow = jax.ShapeDtypeStruct((slots, samples, rows, width), BF16)
    wide = jax.ShapeDtypeStruct((slots, samples, rows, hidden_width), BF16)
    return (
        narrow,
        narrow,
        wide,
        wide,
        jax.ShapeDtypeStruct((samples, slots, 2 * width), F32),
        jax.ShapeDtypeStruct((samples, rows, width), BF16),
    )


def layer_scratch(slots, rows, width, hidden_width):
    return [
        pltpu.VMEM((slots, rows, width), BF16),
        pltpu.VMEM((slots, rows, width), BF16),
        pltpu.VMEM((slots, rows, hidden_width), BF16),
        pltpu.VMEM((slots, rows, hidden_width), BF16),
        pltpu.VMEM((slots, 2 * width), F32),
        pltpu.VMEM((rows, width), BF16),
    ]


def backward_kernel(tick, has_top, has_skip, samples, slots, sections, width, *refs):
    refs = list(refs)
    scal, mod, incoming, up, down, skip_weight, states, pres = refs[:8]
    del refs[:8]
    top = refs.pop(0) if has_top else None
    skip_grad = refs.pop(0) if has_skip else None
    del refs[:6]
    out, *targets = refs[:7]
    gv, hv, modv, upv, downv, skwv, statev, prev, acc, *layers, sems = refs[7:]
    stage, count = scal[0], scal[1]
    sample = tick - 2 * (sections - 1 - stage)
    half = sections // 2

    @pl.when((sample >= 0) & (sample < samples) & (stage != sections - 1))
    def _():
        copy_incoming = pltpu.make_async_copy(incoming, gv, sems.at[0])
        copy_mod = pltpu.make_async_copy(mod.at[sample], modv, sems.at[1])
        copy_skw = pltpu.make_async_copy(skip_weight, skwv, sems.at[2])

        def copy(group, j, source, target):
            return pltpu.make_async_copy(source, target, sems.at[4 + group * slots + j])

        def loads(j):
            return (
                copy(0, j, down.at[j], downv.at[j]),
                copy(1, j, pres.at[sample, j], prev.at[j]),
                copy(2, j, up.at[j], upv.at[j]),
                copy(3, j, states.at[sample, j], statev.at[j]),
            )

        if has_top:
            copy_top = pltpu.make_async_copy(top, gv, sems.at[0])

            @pl.when(stage == sections - 2)
            def _():
                copy_top.start()

            @pl.when(stage != sections - 2)
            def _():
                copy_incoming.start()

        else:
            copy_incoming.start()
        if has_skip:
            copy_skip = pltpu.make_async_copy(skip_grad, hv, sems.at[3])

            @pl.when(stage == 0)
            def _():
                copy_skip.start()

        copy_mod.start()
        decoder = stage >= half

        @pl.loop(0, count)
        def _(i):
            for load in loads(count - 1 - i):
                load.start()

        @pl.when(decoder)
        def _():
            copy_skw.start()

        copy_incoming.wait()
        if has_skip:

            @pl.when(stage == 0)
            def _():
                copy_skip.wait()
                acc[...] = (gv[...] + hv[...]).astype(F32)

            @pl.when(stage != 0)
            def _():
                acc[...] = gv[...].astype(F32)

        else:
            acc[...] = gv[...].astype(F32)
        copy_mod.wait()
        first, finish = backward_layers(
            count,
            sample,
            slots,
            width,
            (modv, upv, downv, statev, prev, acc, *layers),
            targets,
            sems,
            4 + 4 * slots,
            loads,
        )
        gv[...] = first

        @pl.when(decoder)
        def _():
            copy_skw.wait()
            gv[...] = first + nt_dot(first, skwv[...]).astype(BF16)

        save_down = pltpu.make_async_copy(gv, out, sems.at[0])
        save_down.start()
        finish()
        save_down.wait()


def backward_call(tick, scal, mod, incoming, up, down, skip_weight, saved, top, skip_grad, kept):
    states, pres, _ = saved
    samples, slots, rows, width = states.shape
    hidden_width = up.shape[2]
    narrow = (rows, width)
    wide = (rows, hidden_width)
    shapes = (jax.ShapeDtypeStruct(narrow, BF16),)
    shapes += kept_shapes(samples, slots, rows, width, hidden_width)
    operands = [scal, mod, incoming, up, down, skip_weight, states, pres]
    if top is not None:
        operands.append(top)
    if skip_grad is not None:
        operands.append(skip_grad)
    aliases = {len(operands) + i: 1 + i for i in range(6)}
    operands += list(kept)
    out = pl.pallas_call(
        functools.partial(
            backward_kernel,
            tick,
            top is not None,
            skip_grad is not None,
            samples,
            slots,
            4,
            width,
        ),
        out_shape=shapes,
        in_specs=[SMEM] + [ANY] * (len(operands) - 1),
        out_specs=(ANY,) * len(shapes),
        input_output_aliases=aliases,
        scratch_shapes=[
            pltpu.VMEM(narrow, BF16),
            pltpu.VMEM(narrow, BF16),
            pltpu.VMEM((slots, 2 * width), F32),
            pltpu.VMEM((slots, width, hidden_width), BF16),
            pltpu.VMEM((slots, width, hidden_width), BF16),
            pltpu.VMEM((width, width), BF16),
            pltpu.VMEM((slots, *narrow), F32),
            pltpu.VMEM((slots, *wide), BF16),
            pltpu.VMEM(narrow, F32),
            *layer_scratch(slots, rows, width, hidden_width),
            pltpu.SemaphoreType.DMA((6 + 8 * slots,)),
        ],
        compiler_params=pltpu.CompilerParams(vmem_limit_bytes=SECTION_VMEM),
        cost_estimate=pl.CostEstimate(
            flops=slots * rows * width * hidden_width * 4,
            bytes_accessed=14_000_000,
            transcendentals=0,
        ),
        name=f"section_backward_{tick}",
    )(*operands)
    return out[0], out[1:]


def time_product(condition, order, mod_grads, slot):
    placed = jnp.dot(condition[...], order[...], preferred_element_type=F32)
    samples, _, lanes = mod_grads.shape
    grads = [mod_grads[sample, slot : slot + 1, :] for sample in range(samples)]
    grads.append(jnp.zeros((condition.shape[0] - samples, lanes), F32))
    return lax.dot_general(
        placed, jnp.concatenate(grads, axis=0), TN, preferred_element_type=F32
    )


def up_grad_kernel(
    scal, norms, dpres, order, condition, mod_grads, mine, theirs, nv, dv, product, packed, sems
):
    count, core = scal[1], scal[2]
    slots = nv.shape[0]
    block, lanes = mine.shape[2:]

    def loads(j):
        return (
            pltpu.make_async_copy(norms.at[j], nv.at[j], sems.at[0, j]),
            pltpu.make_async_copy(dpres.at[j], dv.at[j], sems.at[1, j]),
        )

    def saves(j):
        place = pl.ds(2 * j, 2)
        return (
            pltpu.make_async_copy(packed.at[1, j], theirs.at[:, place], sems.at[2, j]),
            pltpu.make_async_copy(packed.at[0, j], mine.at[:, place], sems.at[3, j]),
        )

    def pack(j):
        for target, side in ((1, 1 - core), (0, core)):
            for i in range(4):
                for half in range(2):
                    low = pl.multiple_of((side * 4 + i) * block, 8)
                    cols = slice(half * lanes, (half + 1) * lanes)
                    packed[target, j, i, half] = product[pl.ds(low, block), cols].astype(BF16)

    @pl.loop(0, count)
    def _(j):
        for load in loads(j):
            load.start()

    for half in range(2):
        product[:, half * lanes : (half + 1) * lanes] = time_product(
            condition, order, mod_grads, half
        )

    pack(slots)
    for save in saves(slots):
        save.start()

    @pl.loop(0, slots)
    def _(j):
        @pl.when(j < count)
        def _():
            for load in loads(j):
                load.wait()
            placed = jnp.dot(nv[j], order[...], preferred_element_type=F32).astype(BF16)
            product[...] = jnp.dot(placed.T, dv[j], preferred_element_type=F32)
            pack(j)

        @pl.when(j >= count)
        def _():
            for target in range(2):
                packed[target, j] = jnp.zeros(packed.shape[2:], BF16)

        for save in saves(j):
            save.start()

    @pl.loop(0, slots + 1)
    def _(j):
        for save in saves(j):
            save.wait()


def up_grad_call(scal, norms, dpres, order, condition, mod_grads):
    slots, rows, width = norms.shape
    hidden_width = dpres.shape[2]
    block = width // 8
    shape = jax.ShapeDtypeStruct((4, 2 * slots + 2, block, hidden_width // 2), BF16)
    return pl.pallas_call(
        up_grad_kernel,
        out_shape=(shape, shape),
        in_specs=[SMEM, ANY, ANY, VMEM, VMEM, VMEM],
        out_specs=(ANY, ANY),
        scratch_shapes=[
            pltpu.VMEM((slots, rows, width), BF16),
            pltpu.VMEM((slots, rows, hidden_width), BF16),
            pltpu.VMEM((width, hidden_width), F32),
            pltpu.VMEM((2, slots + 1, 4, 2, block, hidden_width // 2), BF16),
            pltpu.SemaphoreType.DMA((4, slots + 1)),
        ],
        compiler_params=pltpu.CompilerParams(vmem_limit_bytes=GRAD_VMEM),
        cost_estimate=pl.CostEstimate(
            flops=2 * slots * rows * width * hidden_width,
            bytes_accessed=12_000_000,
            transcendentals=0,
        ),
        name="up_grad",
    )(scal, norms, dpres, order, condition, mod_grads)


def down_grad_kernel(
    scal,
    hiddens,
    outs,
    skips,
    firsts,
    order,
    condition,
    mod_grads,
    mine,
    theirs,
    hv,
    gv,
    sv,
    fv,
    product,
    prod_time,
    prod_skip,
    packed,
    sems,
):
    stage, count, core = scal[0], scal[1], scal[2]
    slots = hv.shape[0]
    block, lanes = mine.shape[2:]
    width = lanes // 2
    load_skip = pltpu.make_async_copy(skips, sv, sems.at[0, slots])
    load_first = pltpu.make_async_copy(firsts, fv, sems.at[1, slots])

    def loads(j):
        return (
            pltpu.make_async_copy(hiddens.at[j], hv.at[j], sems.at[0, j]),
            pltpu.make_async_copy(outs.at[j], gv.at[j], sems.at[1, j]),
        )

    def saves(j):
        place = pl.ds(2 * j, 2)
        return (
            pltpu.make_async_copy(packed.at[1, j], theirs.at[:, place], sems.at[2, j]),
            pltpu.make_async_copy(packed.at[0, j], mine.at[:, place], sems.at[3, j]),
        )

    @pl.when(stage >= 2)
    def _():
        load_skip.start()
        load_first.start()

    @pl.loop(0, count)
    def _(j):
        for load in loads(j):
            load.start()

    prod_time[...] = time_product(condition, order, mod_grads, slots - 1)
    prod_skip[...] = jnp.zeros_like(prod_skip)

    @pl.when(stage >= 2)
    def _():
        load_skip.wait()
        load_first.wait()
        placed = jnp.dot(sv[...], order[...], preferred_element_type=F32).astype(BF16)
        prod_skip[:, :width] = lax.dot_general(placed, fv[...], TN, preferred_element_type=F32)

    for target, side in ((1, 1 - core), (0, core)):
        for y in range(4):
            low = pl.multiple_of((side * 4 + y) * block, 8)
            packed[target, slots, y, 0] = prod_time[pl.ds(low, block), :].astype(BF16)
            packed[target, slots, y, 1] = prod_skip[pl.ds(low, block), :].astype(BF16)
    for save in saves(slots):
        save.start()

    @pl.loop(0, slots)
    def _(j):
        @pl.when(j < count)
        def _():
            for load in loads(j):
                load.wait()
            for start in range(0, hv.shape[2], CHUNK):
                cols = slice(start, start + CHUNK)
                product[cols, :] = lax.dot_general(
                    hv[j, :, cols], gv[j], TN, preferred_element_type=F32
                )
            for target, side in ((1, 1 - core), (0, core)):
                for y in range(4):
                    for pair in range(2):
                        low = pl.multiple_of((8 * y + 4 * pair + side) * block, 8)
                        high = pl.multiple_of((8 * y + 4 * pair + 2 + side) * block, 8)
                        packed[target, j, y, pair] = jnp.concatenate(
                            [product[pl.ds(low, block), :], product[pl.ds(high, block), :]],
                            axis=1,
                        ).astype(BF16)

        @pl.when(j >= count)
        def _():
            for target in range(2):
                packed[target, j] = jnp.zeros(packed.shape[2:], BF16)

        for save in saves(j):
            save.start()

    @pl.loop(0, slots + 1)
    def _(j):
        for save in saves(j):
            save.wait()


def down_grad_call(scal, hiddens, outs, skips, firsts, order, condition, mod_grads):
    slots, rows, hidden_width = hiddens.shape
    width = outs.shape[2]
    block = width // 8
    shape = jax.ShapeDtypeStruct((4, 2 * slots + 2, block, 2 * width), BF16)
    return pl.pallas_call(
        down_grad_kernel,
        out_shape=(shape, shape),
        in_specs=[SMEM, ANY, ANY, ANY, ANY, VMEM, VMEM, VMEM],
        out_specs=(ANY, ANY),
        scratch_shapes=[
            pltpu.VMEM((slots, rows, hidden_width), BF16),
            pltpu.VMEM((slots, rows, width), BF16),
            pltpu.VMEM((rows, width), BF16),
            pltpu.VMEM((rows, width), BF16),
            pltpu.VMEM((hidden_width, width), F32),
            pltpu.VMEM((width, 2 * width), F32),
            pltpu.VMEM((width, 2 * width), F32),
            pltpu.VMEM((2, slots + 1, 4, 2, block, 2 * width), BF16),
            pltpu.SemaphoreType.DMA((4, slots + 1)),
        ],
        compiler_params=pltpu.CompilerParams(vmem_limit_bytes=GRAD_VMEM),
        cost_estimate=pl.CostEstimate(
            flops=2 * slots * rows * width * hidden_width,
            bytes_accessed=12_000_000,
            transcendentals=0,
        ),
        name="down_grad",
    )(scal, hiddens, outs, skips, firsts, order, condition, mod_grads)


def block_order(width, first, second):
    block = width // 32
    matrix = np.zeros((width, width), ml_dtypes.bfloat16)
    for y in range(4):
        for x in range(4):
            for core in range(2):
                where = {"x": x, "y": y}
                place = (core * 4 + where[first]) * 4 + where[second]
                source = 8 * y + 2 * x + core
                for r in range(block):
                    matrix[source * block + r, place * block + r] = 1
    return jnp.asarray(matrix)


def shifted(size, distance):
    return [(i, (i + distance) % size) for i in range(size)]


def paired(pieces, axis):
    index = lax.axis_index(axis)
    other = 3 - index
    sent = jnp.stack([pieces(index ^ 1), pieces(other ^ 1)])
    arrived = lax.ppermute(sent, axis, [(i, i ^ 1) for i in range(4)])
    passed = add(pieces(other), arrived[1])
    last = lax.ppermute(passed, axis, [(i, 3 - i) for i in range(4)])
    return pieces(index).astype(F32) + arrived[0].astype(F32) + last.astype(F32)


def halved(pieces, axis):
    size = lax.axis_size(axis)
    index = lax.axis_index(axis)
    own, ahead, across, behind = (pieces(lax.rem(index + d, size)) for d in (0, 1, 2, 3))
    cut = own.shape[0] // 2
    forward, backward = shifted(size, 1), shifted(size, size - 1)
    from_behind = lax.ppermute(jnp.concatenate([across[:cut], ahead[cut:]]), axis, forward)
    from_ahead = lax.ppermute(jnp.concatenate([across[cut:], behind[:cut]]), axis, backward)
    rest = own.shape[0] - cut
    passed_on = lax.ppermute(add(ahead[:cut], from_behind[:cut]), axis, forward)
    passed_back = lax.ppermute(add(behind[cut:], from_ahead[:rest]), axis, backward)
    low = add(own[:cut], from_ahead[rest:], passed_on)
    high = add(own[cut:], from_behind[cut:], passed_back)
    return jnp.concatenate([low, high])


def add(*terms):
    total = terms[0].astype(F32)
    for term in terms[1:]:
        total = total + term.astype(F32)
    return total.astype(BF16)


def take(value, index, dim):
    return lax.dynamic_index_in_dim(value, index, dim, keepdims=False)


def per_device(
    latents, cotangent, timesteps, layer_count, up_weight, down_weight, time_weight, skip_weight
):
    sections = lax.axis_size("pipe")
    stage = lax.axis_index("pipe")
    core = lax.axis_index("core")
    samples, rows, width = latents.shape
    up, down, skip_mat = up_weight[0], down_weight[0].swapaxes(1, 2), skip_weight[0]
    slots, _, hidden_width = up.shape
    scal = jnp.stack([stage, layer_count[0], core, core]).astype(jnp.int32)
    condition = jax.nn.silu(embedding(timesteps, width // 2)).astype(BF16)
    modulation = jnp.einsum("mt,jtc->mjc", condition, time_weight[0], preferred_element_type=F32)
    order_x = block_order(width, "x", "y")
    order_y = block_order(width, "y", "x")

    padded = jnp.concatenate([condition, jnp.zeros((16 - samples, width), BF16)])

    lead = 2 * (sections - 1)
    ticks = samples + lead
    empty = jnp.zeros((rows, width), BF16)
    moved, skips_moved, tops, skip_grads = {}, {}, {}, {}
    saved, kept = None, None

    def forward(tick, incoming, skip_in=None):
        return forward_call(
            tick,
            scal,
            modulation,
            latents,
            incoming,
            up,
            down,
            skip_mat,
            skip_in,
            cotangent,
            saved,
            kept,
        )

    for tick in range(lead + 1):
        sent, saved, _, _ = forward(tick, moved.get(tick - 2, empty))
        pairs = [(z, z + 1) for z in range(sections - 1) if 0 <= tick - 2 * z < samples]
        moved[tick] = lax.ppermute(sent, "pipe", pairs)
        if tick < samples:
            skips_moved[tick] = lax.ppermute(sent, "pipe", [(0, sections - 1)])
    for sample in range(samples):
        sent, saved, sent_skip, kept = forward(
            lead + sample, moved[lead - 2 + sample], skips_moved[sample]
        )
        tops[sample] = lax.ppermute(sent, "pipe", [(sections - 1, sections - 2)])
        skip_grads[sample] = lax.ppermute(sent_skip[0], "pipe", [(sections - 1, 0)])
    skips = saved[2]

    moved = {}
    for tick in range(2, ticks):
        incoming, top = moved.get(tick - 2), tops.get(tick - 2)
        if incoming is None:
            incoming, top = top, None
        sent, kept = backward_call(
            tick,
            scal,
            modulation,
            incoming,
            up,
            down,
            skip_mat,
            saved,
            top,
            skip_grads.get(tick - lead),
            kept,
        )
        pairs = [
            (z, z - 1)
            for z in range(1, sections - 1)
            if 0 <= tick - 2 * (sections - 1 - z) < samples
        ]
        if pairs:
            moved[tick] = lax.ppermute(sent, "pipe", pairs)
    norms, outs, hiddens, dpres, mod_grads, firsts = kept
    total_rows = samples * rows

    mine_up, theirs_up = up_grad_call(
        scal,
        norms.reshape(slots, total_rows, width),
        dpres.reshape(slots, total_rows, hidden_width),
        order_x,
        padded,
        mod_grads,
    )
    other_up = lax.ppermute(theirs_up, "core", [(0, 1), (1, 0)])
    mine_down, theirs_down = down_grad_call(
        scal,
        hiddens.reshape(slots, total_rows, hidden_width),
        outs.reshape(slots, total_rows, width),
        skips.reshape(total_rows, width),
        firsts.reshape(total_rows, width),
        order_y,
        padded,
        mod_grads,
    )
    other_down = lax.ppermute(theirs_down, "core", [(0, 1), (1, 0)])

    sum_up = halved(lambda i: add(take(mine_up, i, 0), take(other_up, i, 0)), "x")
    sum_down = halved(lambda i: add(take(mine_down, i, 0), take(other_down, i, 0)), "y")
    block, part = width // 8, width // 32
    blocks = 2 * slots
    down_part = sum_down[:blocks].reshape(slots, 2, block, 2, width).transpose(1, 3, 0, 2, 4)
    down_part = down_part.reshape(4, slots * block, width)
    time_part = sum_down[blocks].reshape(4, part, 2, width).transpose(0, 2, 1, 3)
    skip_part = sum_down[blocks + 1, :, :width].reshape(4, part, width)
    down_part = jnp.concatenate(
        [down_part, time_part.reshape(4, 2 * part, width), skip_part], axis=1
    )
    up_part = sum_up.reshape(blocks + 2, 4, part, 2 * width)

    final_up = paired(lambda i: take(up_part, i, 1), "y")
    final_down = paired(lambda i: take(down_part, i, 0), "x")
    grad_up = final_up[:blocks].reshape(slots, 2, part, 2 * width).transpose(0, 2, 1, 3)
    grad_up = grad_up.reshape(slots, part, hidden_width)
    grad_down = final_down[: slots * block].reshape(slots, block, width)
    last_time = final_down[slots * block : slots * block + 2 * part].reshape(2, part, width)
    last_time = last_time.transpose(1, 0, 2).reshape(1, part, 2 * width)
    grad_time = jnp.concatenate([final_up[blocks:], last_time])
    grad_skip = final_down[slots * block + 2 * part :]
    return (grad_up[None], grad_down[None], grad_time[None], grad_skip[None])


def solution(mesh):
    split = Mesh(
        mesh.devices.reshape(4, 4, 2, mesh.devices.shape[1]), ("y", "x", "core", "pipe")
    )
    dp = ("y", "x", "core")
    placed = (
        P(dp, None, None),
        P(dp, None, None),
        P(dp),
        P("pipe"),
        P("pipe", None, None, None),
        P("pipe", None, None, None),
        P("pipe", None, None, None),
        P("pipe", None, None),
    )
    return jax.shard_map(
        per_device,
        mesh=split,
        in_specs=placed,
        out_specs=(
            P("pipe", None, dp, None),
            P("pipe", None, dp, None),
            P("pipe", None, dp, None),
            P("pipe", dp, None),
        ),
        check_vma=False,
    )
```
